768 devices in a mesh: row: 32 (over y_hi, x, core), col: 24 (over z, y_lo).
Axes of the slice: x: 4, y: 8 (y_hi: 4, y_lo: 2; y = y_hi * 2 + y_lo), z: 12, core: 2. Of those that a mesh axis runs over, the one named last changes fastest.
Arguments:
- tiles: bfloat16 [32, 24, 128, 128, 128], P('row', 'col'), may hold values from -0.09375 to 0.09375
- tile_row: int32 [32, 24, 128], P('row', 'col'), may hold values from 0 to 191
- tile_col: int32 [32, 24, 128], P('row', 'col'), may hold values from 0 to 255
- basis: float32 [8, 786432], P(None, ('row', 'col')), may hold values from -240 to 240
- basis_image: float32 [8, 786432], P(None, ('row', 'col')), may hold values from -240 to 240
- search: float32 [8, 786432], P(None, ('row', 'col')), may hold values from -240 to 240
- search_image: float32 [8, 786432], P(None, ('row', 'col')), may hold values from -240 to 240
- ritz_values: float32 [8], replicated, may hold values from -3 to 3
Outputs:
- ritz_basis: float32 [24, 786432], P(None, ('row', 'col'))
- ritz_images: float32 [24, 786432], P(None, ('row', 'col'))
- projected: float32 [24, 24], replicated
The draws below stay inside these ranges and needn't reach their ends.
All inputs are finite; a program needn't handle non-finite values.
Results may differ from the reference program's by a relative error of at most 0.0021.
Values may be sent and summed in bfloat16 or wider, within the bound.
A program may use at most 32 MiB of HBM per device.

```python
import jax
import jax.numpy as jnp
from jax import lax

TILE = 128
VECS = 8
PIECE = 1024
TILES = 128
PIECE_TILES = 8
DIM = 786432
N_ROW = 32
N_COL = 24


diagonal_level = 0.09375


def shaped(key, base, trend):
    keys = jax.random.split(key, 2)
    vector_scale = jnp.exp(jax.random.uniform(keys[0], (VECS, 1), jnp.float32, -1.15, 1.15))
    blocks = DIM // 128
    block_scale = jnp.exp(jax.random.uniform(keys[1], (VECS, blocks, 1), jnp.float32, -1.15, 1.15))
    block_scale = jnp.broadcast_to(block_scale, (VECS, blocks, 128)).reshape(VECS, DIM)
    position = jnp.arange(DIM, dtype=jnp.float32) / DIM
    rising = jnp.exp(jnp.log(jnp.float32(trend)) * position)
    return (base * vector_scale * block_scale * rising[None, :]).astype(jnp.float32)


def make_vector(key):
    first, second = jax.random.split(key)
    base = jnp.clip(jax.random.normal(first, (VECS, DIM), jnp.float32), -4.0, 4.0)
    return shaped(second, base, 3.0)


def draw_basis(key, part):
    key = jax.random.fold_in(key, 11)
    return make_vector(key)


def draw_basis_image(key, part):
    key = jax.random.fold_in(key, 23)
    return make_vector(key)


def draw_search(key, part):
    key = jax.random.fold_in(key, 37)
    return make_vector(key)


def draw_search_image(key, part):
    key = jax.random.fold_in(key, 41)
    return make_vector(key)


def draw_tiles(key, part):
    key = jax.random.fold_in(key, 53)
    spread = (PIECE / (2.0 * TILES)) ** 0.5 / TILE
    identity = jnp.eye(TILE, dtype=jnp.bool_)
    own_tile = (jnp.arange(TILES, dtype=jnp.int32) < PIECE_TILES)[:, None, None]
    on_diagonal = jnp.logical_and(identity[None, :, :], own_tile)[None]

    def one_group(group):
        group_key = jax.random.fold_in(key, group)
        values = jax.random.normal(group_key, (N_COL, TILES, TILE, TILE), jnp.float32) * spread
        values = jnp.clip(values, -diagonal_level, diagonal_level)
        values = jnp.where(on_diagonal, jnp.float32(diagonal_level), values)
        return values.astype(jnp.bfloat16)
    return lax.map(one_group, jnp.arange(N_ROW, dtype=jnp.int32))


def draw_tile_row(key, part):
    key = jax.random.fold_in(key, 61)
    drawn = jax.random.randint(key, (N_ROW, N_COL, TILES), 0, N_COL * PIECE_TILES, dtype=jnp.int32)
    column = jnp.arange(N_COL, dtype=jnp.int32)[None, :, None]
    slot = jnp.arange(TILES, dtype=jnp.int32)[None, None, :]
    return jnp.where(slot < PIECE_TILES, column * PIECE_TILES + slot, drawn).astype(jnp.int32)


def draw_tile_col(key, part):
    key = jax.random.fold_in(key, 67)
    drawn = jax.random.randint(key, (N_ROW, N_COL, TILES), 0, N_ROW * PIECE_TILES, dtype=jnp.int32)
    row_number = jnp.arange(N_ROW, dtype=jnp.int32)[:, None, None]
    slot = jnp.arange(TILES, dtype=jnp.int32)[None, None, :]
    return jnp.where(slot < PIECE_TILES, row_number * PIECE_TILES + slot, drawn).astype(jnp.int32)


def setup_inputs(seed: int = 0) -> dict:
    arg_keys = jax.random.split(jax.random.key(seed), 9)
    return {
        "tiles": draw_tiles(jax.random.fold_in(arg_keys[8], 71), 0),
        "tile_row": draw_tile_row(jax.random.fold_in(arg_keys[8], 71), 0),
        "tile_col": draw_tile_col(jax.random.fold_in(arg_keys[8], 71), 0),
        "basis": draw_basis(jax.random.fold_in(arg_keys[8], 71), 0),
        "basis_image": draw_basis_image(jax.random.fold_in(arg_keys[8], 71), 0),
        "search": draw_search(jax.random.fold_in(arg_keys[8], 71), 0),
        "search_image": draw_search_image(jax.random.fold_in(arg_keys[8], 71), 0),
        "ritz_values": jnp.clip(jax.random.uniform(arg_keys[7], (VECS,), jnp.float32, -3.0, 3.0), -3.0, 3.0),
    }


def factor(gram):
    size = gram.shape[0]
    lower = jnp.zeros_like(gram)
    index = jnp.arange(size)
    for step in range(size):
        column = gram[:, step] - lax.optimization_barrier(jnp.sum(lower * lower[step][None, :], axis=1))
        pivot = jnp.sqrt(column[step])
        column = jnp.where(index >= step, column / pivot, jnp.float32(0.0))
        lower = lower.at[:, step].set(column)
    return lower

def invert(lower):
    size = lower.shape[0]
    identity = jnp.eye(size, dtype=lower.dtype)
    inverse = jnp.zeros_like(lower)
    for step in range(size):
        solved = (identity[step] - lax.optimization_barrier(jnp.sum(lower[step][:, None] * inverse, axis=0))) / lower[step, step]
        inverse = inverse.at[step].set(solved)
    return inverse

def reference(tiles, tile_row, tile_col, basis, basis_image, search, search_image, ritz_values):
    residual = basis_image - ritz_values[:, None] * basis
    count = DIM // TILE
    lowered = residual.astype(jnp.bfloat16).reshape(VECS, count, TILE)
    columns_index = jnp.arange(N_COL, dtype=jnp.int32)[:, None]

    def one_group(total, inputs):
        group, block, rows, cols = inputs
        global_row = (group * N_COL + rows // PIECE_TILES) * PIECE_TILES + rows % PIECE_TILES
        global_col = (cols // PIECE_TILES * N_COL + columns_index) * PIECE_TILES + cols % PIECE_TILES
        global_row = global_row.reshape(-1).astype(jnp.int32)
        global_col = global_col.reshape(-1).astype(jnp.int32)
        flat = block.reshape(-1, TILE, TILE).astype(jnp.float32)
        col_vals = lowered[:, global_col].astype(jnp.float32)
        row_vals = lowered[:, global_row].astype(jnp.float32)
        forward = jnp.einsum('kij,vkj->kvi', flat, col_vals)
        backward = jnp.einsum('kij,vki->kvj', flat, row_vals)
        total = total + jax.ops.segment_sum(forward, global_row, count)
        total = total + jax.ops.segment_sum(backward, global_col, count)
        return (total, None)
    start = jnp.zeros((count, VECS, TILE), jnp.float32)
    summed, _ = lax.scan(one_group, start, (jnp.arange(N_ROW, dtype=jnp.int32), tiles, tile_row, tile_col))
    residual_image = summed.transpose(1, 0, 2).reshape(VECS, DIM)
    stack = jnp.concatenate([basis, residual, search], axis=0)
    images = jnp.concatenate([basis_image, residual_image, search_image], axis=0)
    highest = lax.Precision.HIGHEST
    gram = jnp.dot(stack, stack.T, precision=highest) / DIM
    raw = jnp.dot(stack, images.T, precision=highest) / DIM
    inverse = invert(factor(gram))
    ritz_basis = jnp.dot(inverse, stack, precision=highest)
    ritz_images = jnp.dot(inverse, images, precision=highest)
    projected = jnp.dot(jnp.dot(inverse, raw, precision=highest), inverse.T, precision=highest)
    return (ritz_basis, ritz_images, projected)
```

```python
import jax
import jax.numpy as jnp
from jax import lax
from jax.experimental import pallas as pl
from jax.experimental.pallas import tpu as pltpu
from jax.sharding import PartitionSpec as P

MESH = pl.DeviceIdType.MESH
TILE = 128
VECS = 8
TILES = 128
N_YH, N_X, N_Z = 4, 4, 12
N_XY = N_YH * N_X
N_ROW, N_COL = 2 * N_XY, 2 * N_Z
F32 = jnp.float32
BF16 = jnp.bfloat16
HIGHEST = lax.Precision.HIGHEST
NT = (((1,), (1,)), ((), ()))
NN = (((1,), (0,)), ((), ()))


def dot_nt(left, right):
    return lax.dot_general(left, right, NT, precision=HIGHEST, preferred_element_type=F32)


def dot_nn(left, right):
    return lax.dot_general(left, right, NN, precision=HIGHEST, preferred_element_type=F32)


def slots_of(index, groups):
    piece, within = index // 8, index % 8
    return ((piece % 2) * groups + piece // 2) * 8 + within


def onehots(ahead, across, slots, count):
    column = jnp.transpose(jnp.broadcast_to(slots.astype(F32), (TILES, TILES)))
    lane = lax.broadcasted_iota(jnp.int32, (TILES, count), 1).astype(F32)
    ahead[...] = (lane == jnp.concatenate([column, column], axis=1)[:, :count]).astype(F32).astype(BF16)
    across[...] = (lax.broadcasted_iota(jnp.int32, (count, TILES), 0) == slots).astype(F32).astype(BF16)


def pick(picked, pieces, ahead, count):
    for m in range(VECS // 2):
        pair = pieces[:, 16 * m:16 * m + 16, :].astype(F32)
        even = pair[:, 0:8, :].reshape(count, TILE).astype(BF16)
        odd = pair[:, 8:16, :].reshape(count, TILE).astype(BF16)
        chosen = lax.dot_general(
            ahead[...], jnp.concatenate([even, odd], axis=1), NN, preferred_element_type=F32
        )
        picked[pl.ds(2 * m, TILES, stride=VECS), :] = chosen[:, :TILE]
        picked[pl.ds(2 * m + 1, TILES, stride=VECS), :] = chosen[:, TILE:]


def place(terms, products, across, count):
    left = jnp.concatenate([across[...], across[...]], axis=1)
    for v in range(0, VECS, 2):
        columns = []
        for u in (v, v + 1):
            values = products[pl.ds(u, TILES, stride=VECS), :]
            high = values.astype(BF16)
            low = (values - high.astype(F32)).astype(BF16)
            columns.append(jnp.concatenate([high, low], axis=0))
        total = lax.dot_general(
            left, jnp.concatenate(columns, axis=1), NN, preferred_element_type=F32
        )
        terms[:, 8 * v:8 * v + 8, :] = total[:, :TILE].reshape(count // 8, 8, TILE)
        terms[:, 8 * v + 8:8 * v + 16, :] = total[:, TILE:].reshape(count // 8, 8, TILE)


def kernel(
    tiles_hbm, row_hbm, col_hbm, basis_hbm, image_hbm, search_hbm, simage_hbm, ritz_hbm,
    ob_hbm, oi_hbm, op_hbm,
    tiles, row_v, col_v, ritz_s, work, images, pieces,
    ahead_r, across_r, ahead_c, across_c, picked_f, picked_b,
    colbuf, rowbuf, products_f, products_b, rowterms, colterms, rowlow, zr, zs, yr,
    csib, csum, cr, ob, oi, opv,
    g_core, g_xy, g_yl, g_z, l_core, l_xy, l_yl, l_z,
    in_sem, out_sem,
    cA_s, cA_r, cB_s, cB_r, zA_s, zA_r, yB_s, yB_r,
    rz_s, rz_r, ry_s, ry_r, sc_s, sc_r, sx_s, sx_r,
    gc_s, gc_r, gx_s, gx_r, gy_s, gy_r, gz_s, gz_r,
    lc_s, lc_r, lx_s, lx_r, ly_s, ly_r, lz_s, lz_r,
):
    row = lax.axis_index("row")
    col = lax.axis_index("col")
    xy, core = row // 2, row % 2
    yh, x = xy // N_X, xy % N_X
    z, yl = col // 2, col % 2
    sibling = (xy * 2 + 1 - core, col)
    across = (row, z * 2 + 1 - yl)

    def plane(dy, dx):
        return (((yh + dy) % N_YH) * N_X + (x + dx) % N_X)

    def plane_from(dy, dx):
        return (((yh + N_YH - dy) % N_YH) * N_X + (x + N_X - dx) % N_X)

    offsets = [(dy, dx) for dy in range(N_YH) for dx in range(N_X)][1:]
    z_order = [6, 5, 7, 4, 8, 3, 9, 2, 10, 1, 11]

    def z_peer(d):
        return (row, ((z + d) % N_Z) * 2 + yl)

    def xy_peer(o):
        return (plane(*o) * 2 + core, col)

    barrier = pltpu.get_barrier_semaphore()
    everyone = [z_peer(d) for d in z_order] + [xy_peer(o) for o in offsets] + [sibling, across]
    for peer in everyone:
        pl.semaphore_signal(barrier, inc=1, device_id=peer, device_id_type=MESH)

    loads = [
        pltpu.make_async_copy(basis_hbm, work.at[pl.ds(0, 8)], in_sem.at[0]),
        pltpu.make_async_copy(image_hbm, work.at[pl.ds(24, 8)], in_sem.at[1]),
        pltpu.make_async_copy(ritz_hbm, ritz_s, in_sem.at[2]),
        pltpu.make_async_copy(search_hbm, work.at[pl.ds(16, 8)], in_sem.at[3]),
        pltpu.make_async_copy(simage_hbm, work.at[pl.ds(32, 8)], in_sem.at[4]),
        pltpu.make_async_copy(row_hbm, row_v, in_sem.at[5]),
        pltpu.make_async_copy(col_hbm, col_v, in_sem.at[6]),
        pltpu.make_async_copy(tiles_hbm.at[0, 0], tiles, in_sem.at[7]),
    ]
    for load in loads:
        load.start()
    for load in loads[:3]:
        load.wait()
    v_index = lax.broadcasted_iota(jnp.int32, (VECS, 1), 0)
    ritz = jnp.zeros((VECS, 1), F32)
    for v in range(VECS):
        ritz = jnp.where(v_index == v, ritz_s[v], ritz)
    residual = work[24:32, :] - ritz * work[0:8, :]
    work[8:16, :] = residual
    mine_col = core * N_XY + xy
    mine_row = yl * N_Z + z
    for t in range(8):
        pieces[pl.ds(t, VECS, stride=8), :] = residual[:, t * TILE:(t + 1) * TILE]
    lowered = pieces[...].astype(BF16)
    colbuf[mine_col] = lowered
    rowbuf[mine_row] = lowered

    pl.semaphore_wait(barrier, len(everyone))

    sends = []

    def remote(src, dst, ss, rs, peer):
        copy = pltpu.make_async_remote_copy(
            src_ref=src, dst_ref=dst, send_sem=ss, recv_sem=rs, device_id=peer, device_id_type=MESH
        )
        return copy

    def send(src, dst, ss, rs, peer):
        copy = remote(src, dst, ss, rs, peer)
        copy.start()
        sends.append(copy)

    def arrived(dst, ss, rs, peer):
        remote(dst, dst, ss, rs, peer).wait_recv()

    for d in z_order:
        send(rowbuf.at[mine_row], rowbuf.at[mine_row], zA_s.at[d], zA_r.at[d], z_peer(d))
    for j, o in enumerate(offsets):
        send(colbuf.at[mine_col], colbuf.at[mine_col], cA_s.at[j], cA_r.at[j], xy_peer(o))
    send(rowbuf.at[mine_row], rowbuf.at[mine_row], yB_s.at[0], yB_r.at[0], across)

    for load in loads[5:7]:
        load.wait()
    onehots(ahead_r, across_r, slots_of(row_v[0], N_Z), N_COL * 8)
    onehots(ahead_c, across_c, slots_of(col_v[0], N_XY), N_ROW * 8)

    for load in loads[3:5]:
        load.wait()
    g_core[core] = jnp.zeros((24, TILE), F32)
    g_core[core, :, 0:40] = dot_nt(work[0:24, :], work[0:40, :])
    send(g_core.at[core], g_core.at[core], gc_s, gc_r, sibling)

    for dy in range(N_YH):
        base = core * N_XY + ((yh + N_YH - dy) % N_YH) * N_X
        for dx in range(N_X):
            if (dy, dx) != (0, 0):
                j = offsets.index((dy, dx))
                here = colbuf.at[core * N_XY + plane_from(dy, dx)]
                arrived(here, cA_s.at[j], cA_r.at[j], xy_peer((dy, dx)))
        block = colbuf.at[pl.ds(base, N_X)]
        send(block, block, cB_s.at[dy], cB_r.at[dy], sibling)
    for d in reversed(z_order):
        here = rowbuf.at[yl * N_Z + (z + N_Z - d) % N_Z]
        arrived(here, zA_s.at[d], zA_r.at[d], z_peer(d))
        send(here, here, yB_s.at[d], yB_r.at[d], across)

    arrived(g_core.at[1 - core], gc_s, gc_r, sibling)
    g_xy[xy] = g_core[0] + g_core[1]
    for j, o in enumerate(offsets):
        send(g_xy.at[xy], g_xy.at[xy], gx_s.at[j], gx_r.at[j], xy_peer(o))

    for dy in range(N_YH):
        block = colbuf.at[pl.ds((1 - core) * N_XY + ((yh + N_YH - dy) % N_YH) * N_X, N_X)]
        arrived(block, cB_s.at[dy], cB_r.at[dy], sibling)
    loads[7].wait()

    def forward(step, carry):
        for u in range(8):
            k = step * 8 + u
            at = pl.ds(pl.multiple_of(k * 8, 8), 8)
            products_f[at, :] = lax.dot_general(
                picked_f[at, :].astype(BF16), tiles[k], NT, preferred_element_type=F32
            )
        return carry

    pick(picked_f, colbuf, ahead_c, N_ROW * 8)
    lax.fori_loop(0, TILES // 8, forward, 0)
    place(rowterms, products_f, across_r, N_COL * 8)
    rowlow[...] = rowterms[...].astype(BF16)
    for h, d in [(h, d) for h in (0, 1) for d in z_order]:
        send(
            rowlow.at[h * N_Z + (z + d) % N_Z], zr.at[h, z], rz_s.at[h, d], rz_r.at[h, d], z_peer(d)
        )

    for j, o in enumerate(offsets):
        arrived(g_xy.at[plane_from(*o)], gx_s.at[j], gx_r.at[j], xy_peer(o))
    total = g_xy[0]
    for j in range(1, N_XY):
        total = total + g_xy[j]
    g_yl[yl] = total
    send(g_yl.at[yl], g_yl.at[yl], gy_s, gy_r, across)

    for d in range(N_Z):
        here = rowbuf.at[(1 - yl) * N_Z + (z + N_Z - d) % N_Z]
        arrived(here, yB_s.at[d], yB_r.at[d], across)

    def backward(step, carry):
        for u in range(8):
            k = step * 8 + u
            at = pl.ds(pl.multiple_of(k * 8, 8), 8)
            products_b[at, :] = lax.dot_general(
                picked_b[at, :].astype(BF16), tiles[k], NN, preferred_element_type=F32
            )
        return carry

    pick(picked_b, rowbuf, ahead_r, N_COL * 8)
    lax.fori_loop(0, TILES // 8, backward, 0)
    place(colterms, products_b, across_c, N_ROW * 8)

    chunk = N_XY // 4
    for q in range(4):
        send(
            colterms.at[pl.ds((1 - core) * N_XY + q * chunk, chunk)],
            csib.at[pl.ds(q * chunk, chunk)], sc_s.at[q], sc_r.at[q], sibling,
        )
    arrived(g_yl.at[1 - yl], gy_s, gy_r, across)
    g_z[z] = g_yl[0] + g_yl[1]
    for d in z_order:
        send(g_z.at[z], g_z.at[z], gz_s.at[d], gz_r.at[d], z_peer(d))
    for q in range(4):
        arrived(csib.at[pl.ds(q * chunk, chunk)], sc_s.at[q], sc_r.at[q], sibling)
    for q in range(N_XY):
        csum[q] = (colterms[core * N_XY + q] + csib[q]).astype(BF16)
    for j, o in enumerate(offsets):
        send(csum.at[plane(*o)], cr.at[xy], sx_s.at[j], sx_r.at[j], xy_peer(o))

    for h, d in [(h, d) for h in (0, 1) for d in z_order]:
        arrived(zr.at[h, (z + N_Z - d) % N_Z], rz_s.at[h, d], rz_r.at[h, d], z_peer(d))

    def over_z(h):
        total = rowterms[h * N_Z + z]
        for d in range(1, N_Z):
            total = total + zr[h, (z + d) % N_Z].astype(F32)
        return total

    zs[0] = over_z(1 - yl)
    send(zs.at[0], yr, ry_s, ry_r, across)
    zs[1] = over_z(yl)

    for d in z_order:
        arrived(g_z.at[(z + N_Z - d) % N_Z], gz_s.at[d], gz_r.at[d], z_peer(d))
    total = g_z[0]
    for j in range(1, N_Z):
        total = total + g_z[j]
    n_total = F32(1024 * N_ROW * N_COL)
    total = total / n_total
    rows = lax.broadcasted_iota(jnp.int32, (24, 24), 0)
    columns = lax.broadcasted_iota(jnp.int32, (24, 24), 1)
    matrix = jnp.concatenate([total[:, 0:24], jnp.where(rows == columns, F32(1.0), F32(0.0))], axis=1)
    index = lax.broadcasted_iota(jnp.int32, (24, 1), 0)
    for step in range(24):
        pivot = jnp.sqrt(matrix[step:step + 1, step:step + 1])
        scaled = matrix[step:step + 1, :] / pivot
        factor = matrix[:, step:step + 1] / pivot
        matrix = jnp.where(
            index == step, scaled, jnp.where(index > step, matrix - factor * scaled, matrix)
        )
    inverse = matrix[:, 24:48]
    given = dot_nt(dot_nn(inverse, total[:, 24:32]), inverse[:, 0:8]) + dot_nt(
        dot_nn(inverse, total[:, 32:40]), inverse[:, 16:24]
    )
    ob[...] = dot_nn(inverse, work[0:24, :])
    store_b = pltpu.make_async_copy(ob, ob_hbm, out_sem.at[0])
    store_b.start()

    arrived(yr, ry_s, ry_r, across)
    image = zs[1] + yr[...] + (colterms[core * N_XY + xy] + csib[xy])
    for j, o in enumerate(offsets):
        here = cr.at[plane_from(*o)]
        arrived(here, sx_s.at[j], sx_r.at[j], xy_peer(o))
        image = image + cr[plane_from(*o)].astype(F32)
    pieces[...] = image
    for t in range(8):
        images[8:16, t * TILE:(t + 1) * TILE] = pieces[pl.ds(t, VECS, stride=8), :]
    images[0:8, :] = work[24:32, :]
    images[16:24, :] = work[32:40, :]

    l_core[core] = jnp.zeros((VECS, TILE), F32)
    l_core[core, :, 0:24] = dot_nt(images[8:16, :], work[0:24, :])
    send(l_core.at[core], l_core.at[core], lc_s, lc_r, sibling)
    arrived(l_core.at[1 - core], lc_s, lc_r, sibling)
    l_xy[xy] = l_core[0] + l_core[1]
    for j, o in enumerate(offsets):
        send(l_xy.at[xy], l_xy.at[xy], lx_s.at[j], lx_r.at[j], xy_peer(o))
    oi[...] = dot_nn(inverse, images[...])
    store_i = pltpu.make_async_copy(oi, oi_hbm, out_sem.at[1])
    store_i.start()
    for j, o in enumerate(offsets):
        arrived(l_xy.at[plane_from(*o)], lx_s.at[j], lx_r.at[j], xy_peer(o))
    late = l_xy[0]
    for j in range(1, N_XY):
        late = late + l_xy[j]
    l_yl[yl] = late
    send(l_yl.at[yl], l_yl.at[yl], ly_s, ly_r, across)
    arrived(l_yl.at[1 - yl], ly_s, ly_r, across)
    l_z[z] = l_yl[0] + l_yl[1]
    for d in z_order:
        send(l_z.at[z], l_z.at[z], lz_s.at[d], lz_r.at[d], z_peer(d))
    for d in z_order:
        arrived(l_z.at[(z + N_Z - d) % N_Z], lz_s.at[d], lz_r.at[d], z_peer(d))
    late = l_z[0]
    for j in range(1, N_Z):
        late = late + l_z[j]
    late = late / n_total
    opv[...] = given + dot_nt(dot_nt(inverse, late[:, 0:24]), inverse[:, 8:16])
    store_p = pltpu.make_async_copy(opv, op_hbm, out_sem.at[2])
    store_p.start()
    for copy in sends:
        copy.wait_send()
    store_b.wait()
    store_i.wait()
    store_p.wait()


def on_device(tiles, tile_row, tile_col, basis, basis_image, search, search_image, ritz_values):
    vmem, dma = pltpu.VMEM, pltpu.SemaphoreType.DMA
    n_off = N_XY - 1
    return tuple(pl.pallas_call(
        kernel,
        out_shape=(
            jax.ShapeDtypeStruct((24, 1024), F32),
            jax.ShapeDtypeStruct((24, 1024), F32),
            jax.ShapeDtypeStruct((24, 24), F32),
        ),
        in_specs=[pl.BlockSpec(memory_space=pl.ANY)] * 8,
        out_specs=[pl.BlockSpec(memory_space=pl.ANY)] * 3,
        scratch_shapes=[
            vmem((TILES, TILE, TILE), BF16),
            vmem((1, 1, TILES), jnp.int32),
            vmem((1, 1, TILES), jnp.int32),
            pltpu.SMEM((VECS,), F32),
            vmem((40, 1024), F32),
            vmem((24, 1024), F32),
            vmem((64, TILE), F32),
            vmem((TILES, N_COL * 8), BF16),
            vmem((N_COL * 8, TILES), BF16),
            vmem((TILES, N_ROW * 8), BF16),
            vmem((N_ROW * 8, TILES), BF16),
            vmem((TILES * VECS, TILE), F32),
            vmem((TILES * VECS, TILE), F32),
            vmem((N_ROW, 64, TILE), BF16),
            vmem((N_COL, 64, TILE), BF16),
            vmem((TILES * VECS, TILE), F32),
            vmem((TILES * VECS, TILE), F32),
            vmem((N_COL, 64, TILE), F32),
            vmem((N_ROW, 64, TILE), F32),
            vmem((N_COL, 64, TILE), BF16),
            vmem((2, N_Z, 64, TILE), BF16),
            vmem((2, 64, TILE), F32),
            vmem((64, TILE), F32),
            vmem((N_XY, 64, TILE), F32),
            vmem((N_XY, 64, TILE), BF16),
            vmem((N_XY, 64, TILE), BF16),
            vmem((24, 1024), F32),
            vmem((24, 1024), F32),
            vmem((24, 24), F32),
            vmem((2, 24, TILE), F32),
            vmem((N_XY, 24, TILE), F32),
            vmem((2, 24, TILE), F32),
            vmem((N_Z, 24, TILE), F32),
            vmem((2, VECS, TILE), F32),
            vmem((N_XY, VECS, TILE), F32),
            vmem((2, VECS, TILE), F32),
            vmem((N_Z, VECS, TILE), F32),
            dma((8,)), dma((3,)),
            dma((n_off,)), dma((n_off,)), dma((N_YH,)), dma((N_YH,)),
            dma((N_Z,)), dma((N_Z,)), dma((N_Z,)), dma((N_Z,)),
            dma((2, N_Z)), dma((2, N_Z)), dma(()), dma(()), dma((4,)), dma((4,)), dma((n_off,)), dma((n_off,)),
            dma(()), dma(()), dma((n_off,)), dma((n_off,)), dma(()), dma(()), dma((N_Z,)), dma((N_Z,)),
            dma(()), dma(()), dma((n_off,)), dma((n_off,)), dma(()), dma(()), dma((N_Z,)), dma((N_Z,)),
        ],
        compiler_params=pltpu.CompilerParams(
            collective_id=0, has_side_effects=True, vmem_limit_bytes=56 * 2**20
        ),
        name="step",
    )(tiles, tile_row, tile_col, basis, basis_image, search, search_image, ritz_values))


def solution(mesh):
    vectors = P(None, ("row", "col"))
    return jax.shard_map(
        on_device,
        mesh=mesh,
        in_specs=(
            P("row", "col", None, None, None),
            P("row", "col", None),
            P("row", "col", None),
            vectors, vectors, vectors, vectors,
            P(),
        ),
        out_specs=(vectors, vectors, P()),
        check_vma=False,
    )
```

```python
import jax
import jax.numpy as jnp
from jax import lax
from jax.experimental import pallas as pl
from jax.experimental.pallas import tpu as pltpu
from jax.sharding import PartitionSpec as P

MESH = pl.DeviceIdType.MESH
TILE = 128
VECS = 8
TILES = 128
N_YH, N_X, N_Z = 4, 4, 12
N_XY = N_YH * N_X
N_ROW, N_COL = 2 * N_XY, 2 * N_Z
F32 = jnp.float32
BF16 = jnp.bfloat16
HIGHEST = lax.Precision.HIGHEST
NT = (((1,), (1,)), ((), ()))
NN = (((1,), (0,)), ((), ()))
Z_ORDER = (6, 5, 7, 4, 8, 3, 9, 2, 10, 1, 11)
OFFSETS = tuple((dy, dx) for dy in range(N_YH) for dx in range(N_X))[1:]


def dot_nt(left, right):
    return lax.dot_general(left, right, NT, precision=HIGHEST, preferred_element_type=F32)


def dot_nn(left, right):
    return lax.dot_general(left, right, NN, precision=HIGHEST, preferred_element_type=F32)


def matmul(left, right, dims):
    return lax.dot_general(left, right, dims, preferred_element_type=F32)


def halves(values):
    high = values.astype(BF16)
    return high, (values - high.astype(F32)).astype(BF16)


def slots_of(index, groups):
    piece, within = index // 8, index % 8
    return ((piece % 2) * groups + piece // 2) * 8 + within


def onehots(ahead, across, slots, count):
    column = jnp.transpose(jnp.broadcast_to(slots.astype(F32), (TILES, TILES)))
    lane = lax.broadcasted_iota(jnp.int32, (TILES, count), 1).astype(F32)
    ahead[...] = (lane == jnp.concatenate([column, column], axis=1)[:, :count]).astype(F32).astype(BF16)
    across[...] = (lax.broadcasted_iota(jnp.int32, (count, TILES), 0) == slots).astype(F32).astype(BF16)


def pick(picked, pieces, ahead, count):
    for m in range(VECS // 2):
        pair = pieces[:, 16 * m:16 * m + 16, :].astype(F32)
        even = pair[:, 0:8, :].reshape(count, TILE).astype(BF16)
        odd = pair[:, 8:16, :].reshape(count, TILE).astype(BF16)
        chosen = matmul(ahead[...], jnp.concatenate([even, odd], axis=1), NN)
        picked[pl.ds(2 * m, TILES, stride=VECS), :] = chosen[:, :TILE]
        picked[pl.ds(2 * m + 1, TILES, stride=VECS), :] = chosen[:, TILE:]


def place(terms, products, across, count):
    left = jnp.concatenate([across[...], across[...]], axis=1)
    for v in range(0, VECS, 2):
        columns = []
        for u in (v, v + 1):
            columns.append(jnp.concatenate(halves(products[pl.ds(u, TILES, stride=VECS), :]), axis=0))
        total = matmul(left, jnp.concatenate(columns, axis=1), NN)
        terms[:, 8 * v:8 * v + 8, :] = total[:, :TILE].reshape(count // 8, 8, TILE)
        terms[:, 8 * v + 8:8 * v + 16, :] = total[:, TILE:].reshape(count // 8, 8, TILE)


def multiply(products, picked, blocks):
    upper = lax.broadcasted_iota(jnp.int32, (16, TILE), 0) < 8

    def step(i, carry):
        for u in range(32):
            k = (i * 32 + u) * 2
            at = pl.ds(pl.multiple_of(k * 8, 16), 16)
            vectors = picked[at, :]
            left = jnp.concatenate(
                [jnp.where(upper, vectors, 0.0), jnp.where(upper, 0.0, vectors)], axis=1
            ).astype(BF16)
            products[at, :] = matmul(left, blocks[pl.ds(k, 2)].reshape(2 * TILE, TILE), NN)
        return carry

    lax.fori_loop(0, TILES // 64, step, 0)


def with_stack(sums, others, own):
    left, first, second = [], [], []
    for p in range(sums.shape[0]):
        for t in range(8):
            left.append(jnp.concatenate(halves(sums[p, pl.ds(t, VECS, stride=8), :]), axis=0))
            first.append(others[p, 16 * t:16 * t + 16, :])
            second.append(own[p, 8 * t:8 * t + 8, :].astype(BF16))
    left = jnp.concatenate(left, axis=1)
    first = matmul(left, jnp.concatenate(first, axis=1), NT)
    second = matmul(left, jnp.concatenate(second, axis=1), NT)
    both = jnp.concatenate([first, second], axis=1)
    return both[0:8] + both[8:16]


def by_tile(out, pieces, scratch):
    for p in range(out.shape[0]):
        scratch[...] = pieces[p].astype(F32)
        for t in range(8):
            out[p, 8 * t:8 * t + 8, :] = scratch[pl.ds(t, VECS, stride=8), :]


def kernel(
    tiles_hbm, row_hbm, col_hbm, basis_hbm, image_hbm, search_hbm, simage_hbm, ritz_hbm,
    ob, oi, opv,
    tiles, turned, row_v, col_v, ritz_s, work, images, pieces, scratch,
    ahead_r, across_r, ahead_c, across_c, picked, products,
    colbuf, rowbuf, others_c, others_r, own_c, own_r,
    rowterms, colterms, rowlow, ysib, rowsum, zlow, zr, csib, colsum, clow, cr,
    g_core, g_xy, g_yl, g_z, l_core, l_xy, l_yl, l_z,
    in_sem,
    cA_s, cA_r, cB_s, cB_r, zA_s, zA_r, yB_s, yB_r,
    oz_s, oz_r, oy_s, oy_r, ox_s, ox_r,
    ry_s, ry_r, rz_s, rz_r, sc_s, sc_r, sx_s, sx_r,
    gc_s, gc_r, gx_s, gx_r, gy_s, gy_r, gz_s, gz_r,
    lc_s, lc_r, lx_s, lx_r, ly_s, ly_r, lz_s, lz_r,
):
    row = lax.axis_index("row")
    col = lax.axis_index("col")
    xy, core = row // 2, row % 2
    yh, x = xy // N_X, xy % N_X
    z, yl = col // 2, col % 2
    sibling = (xy * 2 + 1 - core, col)
    across = (row, z * 2 + 1 - yl)

    def plane(dy, dx):
        return ((yh + dy) % N_YH) * N_X + (x + dx) % N_X

    def z_at(d):
        return (z + d) % N_Z

    def z_peer(d):
        return (row, z_at(d) * 2 + yl)

    def xy_peer(o):
        return (plane(*o) * 2 + core, col)

    def xy_from(o):
        return plane(N_YH - o[0], N_X - o[1])

    barrier = pltpu.get_barrier_semaphore()
    everyone = [z_peer(d) for d in Z_ORDER] + [xy_peer(o) for o in OFFSETS] + [sibling, across]
    for peer in everyone:
        pl.semaphore_signal(barrier, inc=1, device_id=peer, device_id_type=MESH)

    loads = [
        pltpu.make_async_copy(basis_hbm, work.at[pl.ds(0, 8)], in_sem.at[0]),
        pltpu.make_async_copy(image_hbm, work.at[pl.ds(24, 8)], in_sem.at[1]),
        pltpu.make_async_copy(ritz_hbm, ritz_s, in_sem.at[2]),
        pltpu.make_async_copy(search_hbm, work.at[pl.ds(16, 8)], in_sem.at[3]),
        pltpu.make_async_copy(simage_hbm, work.at[pl.ds(32, 8)], in_sem.at[4]),
        pltpu.make_async_copy(row_hbm, row_v, in_sem.at[5]),
        pltpu.make_async_copy(col_hbm, col_v, in_sem.at[6]),
        pltpu.make_async_copy(tiles_hbm.at[0, 0], tiles, in_sem.at[7]),
    ]
    for load in loads:
        load.start()
    for load in loads[:4]:
        load.wait()
    v_index = lax.broadcasted_iota(jnp.int32, (VECS, 1), 0)
    ritz = jnp.zeros((VECS, 1), F32)
    for v in range(VECS):
        ritz = jnp.where(v_index == v, ritz_s[v], ritz)
    residual = work[24:32, :] - ritz * work[0:8, :]
    work[8:16, :] = residual
    mine_col = core * N_XY + xy
    mine_row = yl * N_Z + z
    for t in range(8):
        cut = slice(t * TILE, (t + 1) * TILE)
        pieces[pl.ds(t, VECS, stride=8), :] = residual[:, cut]
        pair = jnp.concatenate([work[0:8, cut], work[16:24, cut]], axis=0).astype(BF16)
        others_c[xy, 16 * t:16 * t + 16, :] = pair
        others_r[z, 16 * t:16 * t + 16, :] = pair
    lowered = pieces[...].astype(BF16)
    colbuf[mine_col] = lowered
    rowbuf[mine_row] = lowered

    pl.semaphore_wait(barrier, len(everyone))

    sends = []

    def remote(src, dst, ss, rs, peer):
        return pltpu.make_async_remote_copy(
            src_ref=src, dst_ref=dst, send_sem=ss, recv_sem=rs, device_id=peer, device_id_type=MESH
        )

    def send(src, dst, ss, rs, peer):
        copy = remote(src, dst, ss, rs, peer)
        copy.start()
        sends.append(copy)

    def arrived(dst, ss, rs, peer):
        remote(dst, dst, ss, rs, peer).wait_recv()

    for d in Z_ORDER:
        send(rowbuf.at[mine_row], rowbuf.at[mine_row], zA_s.at[d], zA_r.at[d], z_peer(d))
    for j, o in enumerate(OFFSETS):
        send(colbuf.at[mine_col], colbuf.at[mine_col], cA_s.at[j], cA_r.at[j], xy_peer(o))
    send(rowbuf.at[mine_row], rowbuf.at[mine_row], yB_s.at[0], yB_r.at[0], across)

    def others_start():
        for d in Z_ORDER:
            send(others_r.at[z], others_r.at[z], oz_s.at[d], oz_r.at[d], z_peer(d))
        for d in (2, 1, 3):
            send(others_c.at[xy], others_c.at[xy], oy_s.at[d], oy_r.at[d], xy_peer((d, 0)))
        for d in (2, 1, 3):
            send(others_c.at[xy], others_c.at[xy], ox_s.at[0, d], ox_r.at[0, d], xy_peer((0, d)))

    others_start()

    for load in loads[5:7]:
        load.wait()
    onehots(ahead_r, across_r, slots_of(row_v[0], N_Z), N_COL * 8)
    onehots(ahead_c, across_c, slots_of(col_v[0], N_XY), N_ROW * 8)

    loads[4].wait()
    given = dot_nt(work[0:24, :], work[0:40, :])
    g_core[core] = jnp.concatenate(
        [given[0:8], given[8:16], given[16:24], jnp.zeros((8, 8), F32)], axis=1
    )
    send(g_core.at[core], g_core.at[core], gc_s, gc_r, sibling)

    loads[7].wait()

    def turn(i, carry):
        for u in range(16):
            turned[i * 16 + u] = tiles[i * 16 + u].T
        return carry

    lax.fori_loop(0, TILES // 16, turn, 0)

    for dy in range(N_YH):
        for dx in range(N_X):
            if (dy, dx) != (0, 0):
                j = OFFSETS.index((dy, dx))
                arrived(colbuf.at[core * N_XY + xy_from((dy, dx))], cA_s.at[j], cA_r.at[j], xy_peer((dy, dx)))
        block = colbuf.at[pl.ds(core * N_XY + ((yh + N_YH - dy) % N_YH) * N_X, N_X)]
        send(block, block, cB_s.at[dy], cB_r.at[dy], sibling)
    for d in reversed(Z_ORDER):
        here = rowbuf.at[yl * N_Z + z_at(N_Z - d)]
        arrived(here, zA_s.at[d], zA_r.at[d], z_peer(d))
        send(here, here, yB_s.at[d], yB_r.at[d], across)

    def others_on():
        for d in (1, 3, 2):
            here = others_c.at[plane(N_YH - d, 0)]
            arrived(here, oy_s.at[d], oy_r.at[d], xy_peer((d, 0)))
            for e in (2, 1, 3):
                send(here, here, ox_s.at[d, e], ox_r.at[d, e], xy_peer((0, e)))

    others_on()
    arrived(g_core.at[1 - core], gc_s, gc_r, sibling)
    g_xy[xy] = g_core[0] + g_core[1]
    for j, o in enumerate(OFFSETS):
        send(g_xy.at[xy], g_xy.at[xy], gx_s.at[j], gx_r.at[j], xy_peer(o))

    for dy in range(N_YH):
        block = colbuf.at[pl.ds((1 - core) * N_XY + ((yh + N_YH - dy) % N_YH) * N_X, N_X)]
        arrived(block, cB_s.at[dy], cB_r.at[dy], sibling)
    pick(picked, colbuf, ahead_c, N_ROW * 8)
    multiply(products, picked, turned)
    place(rowterms, products, across_r, N_COL * 8)
    for q in range(2):
        half = pl.ds(q * N_Z // 2, N_Z // 2)
        rowlow[half] = rowterms[pl.ds((1 - yl) * N_Z + q * N_Z // 2, N_Z // 2)].astype(BF16)
        send(rowlow.at[half], ysib.at[half], ry_s.at[q], ry_r.at[q], across)

    for d in range(N_Z):
        arrived(rowbuf.at[(1 - yl) * N_Z + z_at(N_Z - d)], yB_s.at[d], yB_r.at[d], across)
    pick(picked, rowbuf, ahead_r, N_COL * 8)
    multiply(products, picked, tiles)
    place(colterms, products, across_c, N_ROW * 8)
    chunk = N_XY // 4
    for q in range(4):
        send(
            colterms.at[pl.ds((1 - core) * N_XY + q * chunk, chunk)],
            csib.at[pl.ds(q * chunk, chunk)], sc_s.at[q], sc_r.at[q], sibling,
        )

    for j, o in enumerate(OFFSETS):
        arrived(g_xy.at[xy_from(o)], gx_s.at[j], gx_r.at[j], xy_peer(o))
    total = g_xy[0]
    for j in range(1, N_XY):
        total = total + g_xy[j]
    g_yl[yl] = total
    send(g_yl.at[yl], g_yl.at[yl], gy_s, gy_r, across)
    by_tile(own_c, colbuf.at[pl.ds(core * N_XY, N_XY)], scratch)
    by_tile(own_r, rowbuf.at[pl.ds(yl * N_Z, N_Z)], scratch)

    for q in range(4):
        at = pl.ds(q * chunk, chunk)
        arrived(csib.at[at], sc_s.at[q], sc_r.at[q], sibling)
        both = colterms[pl.ds(core * N_XY + q * chunk, chunk)] + csib[at]
        colsum[at] = both
        clow[at] = both.astype(BF16)
    for j, o in enumerate(OFFSETS):
        send(clow.at[plane(*o)], cr.at[xy], sx_s.at[j], sx_r.at[j], xy_peer(o))
    arrived(g_yl.at[1 - yl], gy_s, gy_r, across)
    g_z[z] = g_yl[0] + g_yl[1]
    for d in Z_ORDER:
        send(g_z.at[z], g_z.at[z], gz_s.at[d], gz_r.at[d], z_peer(d))
    for q in range(2):
        half = pl.ds(q * N_Z // 2, N_Z // 2)
        arrived(ysib.at[half], ry_s.at[q], ry_r.at[q], across)
        both = rowterms[pl.ds(yl * N_Z + q * N_Z // 2, N_Z // 2)] + ysib[half].astype(F32)
        rowsum[half] = both
        zlow[half] = both.astype(BF16)
    for d in Z_ORDER:
        send(zlow.at[z_at(d)], zr.at[z], rz_s.at[d], rz_r.at[d], z_peer(d))
    for d in (1, 2, 3):
        for e in range(N_YH):
            arrived(others_c.at[plane(N_YH - e, N_X - d)], ox_s.at[e, d], ox_r.at[e, d], xy_peer((0, d)))
    in_plane = with_stack(colsum, others_c, own_c)
    for d in Z_ORDER:
        arrived(others_r.at[z_at(N_Z - d)], oz_s.at[d], oz_r.at[d], z_peer(d))
    l_core[core] = jnp.zeros((VECS, TILE), F32)
    l_core[core, :, 0:24] = in_plane + with_stack(rowsum, others_r, own_r)
    send(l_core.at[core], l_core.at[core], lc_s, lc_r, sibling)
    arrived(l_core.at[1 - core], lc_s, lc_r, sibling)
    l_xy[xy] = l_core[0] + l_core[1]
    for j, o in enumerate(OFFSETS):
        send(l_xy.at[xy], l_xy.at[xy], lx_s.at[j], lx_r.at[j], xy_peer(o))

    for d in Z_ORDER:
        arrived(g_z.at[z_at(N_Z - d)], gz_s.at[d], gz_r.at[d], z_peer(d))
    total = g_z[0]
    for j in range(1, N_Z):
        total = total + g_z[j]
    n_total = F32(1024 * N_ROW * N_COL)
    total = total / n_total
    total = jnp.concatenate([total[:, 0:40], total[:, 40:80], total[:, 80:120]], axis=0)
    rows = lax.broadcasted_iota(jnp.int32, (24, 24), 0)
    columns = lax.broadcasted_iota(jnp.int32, (24, 24), 1)
    matrix = jnp.concatenate([total[:, 0:24], jnp.where(rows == columns, F32(1.0), F32(0.0))], axis=1)
    index = lax.broadcasted_iota(jnp.int32, (24, 1), 0)
    for step in range(24):
        pivot = jnp.sqrt(matrix[step:step + 1, step:step + 1])
        scaled = matrix[step:step + 1, :] / pivot
        factor = matrix[:, step:step + 1] / pivot
        matrix = jnp.where(
            index == step, scaled, jnp.where(index > step, matrix - factor * scaled, matrix)
        )
    inverse = matrix[:, 24:48]
    reordered = jnp.concatenate([inverse[:, 0:8], inverse[:, 16:24], inverse[:, 8:16]], axis=1)
    given = dot_nt(dot_nn(inverse, total[:, 24:32]), inverse[:, 0:8]) + dot_nt(
        dot_nn(inverse, total[:, 32:40]), inverse[:, 16:24]
    )
    ob[...] = dot_nn(inverse, work[0:24, :])

    for j, o in enumerate(OFFSETS):
        arrived(l_xy.at[xy_from(o)], lx_s.at[j], lx_r.at[j], xy_peer(o))
    late = l_xy[0]
    for j in range(1, N_XY):
        late = late + l_xy[j]
    l_yl[yl] = late
    send(l_yl.at[yl], l_yl.at[yl], ly_s, ly_r, across)
    arrived(l_yl.at[1 - yl], ly_s, ly_r, across)
    l_z[z] = l_yl[0] + l_yl[1]
    for d in Z_ORDER:
        send(l_z.at[z], l_z.at[z], lz_s.at[d], lz_r.at[d], z_peer(d))

    image = rowsum[z] + colsum[xy]
    for d in reversed(Z_ORDER):
        arrived(zr.at[z_at(N_Z - d)], rz_s.at[d], rz_r.at[d], z_peer(d))
        image = image + zr[z_at(N_Z - d)].astype(F32)
    for j, o in enumerate(OFFSETS):
        arrived(cr.at[xy_from(o)], sx_s.at[j], sx_r.at[j], xy_peer(o))
        image = image + cr[xy_from(o)].astype(F32)
    pieces[...] = image
    for t in range(8):
        images[8:16, t * TILE:(t + 1) * TILE] = pieces[pl.ds(t, VECS, stride=8), :]
    images[0:8, :] = work[24:32, :]
    images[16:24, :] = work[32:40, :]
    oi[...] = dot_nn(inverse, images[...])

    for d in Z_ORDER:
        arrived(l_z.at[z_at(N_Z - d)], lz_s.at[d], lz_r.at[d], z_peer(d))
    late = l_z[0]
    for j in range(1, N_Z):
        late = late + l_z[j]
    late = late / n_total
    opv[...] = given + dot_nt(dot_nt(reordered, late[:, 0:24]), inverse[:, 8:16])
    for copy in sends:
        copy.wait_send()


def on_device(tiles, tile_row, tile_col, basis, basis_image, search, search_image, ritz_values):
    vmem, dma = pltpu.VMEM, pltpu.SemaphoreType.DMA
    n_off = N_XY - 1
    outs = (
        jax.ShapeDtypeStruct((24, 1024), F32),
        jax.ShapeDtypeStruct((24, 1024), F32),
        jax.ShapeDtypeStruct((24, 24), F32),
    )

    def pairs(*shapes):
        return [dma(shape) for shape in shapes for _ in range(2)]

    results = pl.pallas_call(
        kernel,
        out_shape=tuple(vmem(out.shape, F32) for out in outs),
        in_specs=[pl.BlockSpec(memory_space=pl.ANY)] * 8,
        out_specs=[pl.BlockSpec(memory_space=vmem)] * 3,
        scratch_shapes=[
            vmem((TILES, TILE, TILE), BF16),
            vmem((TILES, TILE, TILE), BF16),
            vmem((1, 1, TILES), jnp.int32),
            vmem((1, 1, TILES), jnp.int32),
            pltpu.SMEM((VECS,), F32),
            vmem((40, 1024), F32),
            vmem((24, 1024), F32),
            vmem((64, TILE), F32),
            vmem((64, TILE), F32),
            vmem((TILES, N_COL * 8), BF16),
            vmem((N_COL * 8, TILES), BF16),
            vmem((TILES, N_ROW * 8), BF16),
            vmem((N_ROW * 8, TILES), BF16),
            vmem((TILES * VECS, TILE), F32),
            vmem((TILES * VECS, TILE), F32),
            vmem((N_ROW, 64, TILE), BF16),
            vmem((N_COL, 64, TILE), BF16),
            vmem((N_XY, 128, TILE), BF16),
            vmem((N_Z, 128, TILE), BF16),
            vmem((N_XY, 64, TILE), F32),
            vmem((N_Z, 64, TILE), F32),
            vmem((N_COL, 64, TILE), F32),
            vmem((N_ROW, 64, TILE), F32),
            vmem((N_Z, 64, TILE), BF16),
            vmem((N_Z, 64, TILE), BF16),
            vmem((N_Z, 64, TILE), F32),
            vmem((N_Z, 64, TILE), BF16),
            vmem((N_Z, 64, TILE), BF16),
            vmem((N_XY, 64, TILE), F32),
            vmem((N_XY, 64, TILE), F32),
            vmem((N_XY, 64, TILE), BF16),
            vmem((N_XY, 64, TILE), BF16),
            vmem((2, 8, TILE), F32),
            vmem((N_XY, 8, TILE), F32),
            vmem((2, 8, TILE), F32),
            vmem((N_Z, 8, TILE), F32),
            vmem((2, 8, TILE), F32),
            vmem((N_XY, 8, TILE), F32),
            vmem((2, 8, TILE), F32),
            vmem((N_Z, 8, TILE), F32),
            dma((8,)),
        ] + pairs(
            (n_off,), (N_YH,), (N_Z,), (N_Z,), (N_Z,), (N_YH,), (N_YH, N_X),
            (2,), (N_Z,), (4,), (n_off,),
            (), (n_off,), (), (N_Z,), (), (n_off,), (), (N_Z,),
        ),
        compiler_params=pltpu.CompilerParams(
            collective_id=0, has_side_effects=True, vmem_limit_bytes=56 * 2**20
        ),
        name="step",
    )(tiles, tile_row, tile_col, basis, basis_image, search, search_image, ritz_values)
    return tuple(results)


def solution(mesh):
    vectors = P(None, ("row", "col"))
    return jax.shard_map(
        on_device,
        mesh=mesh,
        in_specs=(
            P("row", "col", None, None, None),
            P("row", "col", None),
            P("row", "col", None),
            vectors, vectors, vectors, vectors,
            P(),
        ),
        out_specs=(vectors, vectors, P()),
        check_vma=False,
    )
```

```python
import jax
import jax.numpy as jnp
from jax import lax
from jax.experimental import pallas as pl
from jax.experimental.pallas import tpu as pltpu
from jax.sharding import PartitionSpec as P

MESH = pl.DeviceIdType.MESH
TILE = 128
VECS = 8
TILES = 128
N_YH, N_X, N_Z = 4, 4, 12
N_XY = N_YH * N_X
N_ROW, N_COL = 2 * N_XY, 2 * N_Z
F32 = jnp.float32
BF16 = jnp.bfloat16
HIGHEST = lax.Precision.HIGHEST
NT = (((1,), (1,)), ((), ()))
NN = (((1,), (0,)), ((), ()))
Z_ORDER = (6, 5, 7, 4, 8, 3, 9, 2, 10, 1, 11)
IN_COL = tuple((d, e) for d in Z_ORDER for e in (0, 1)) + ((0, 1),)
OFFSETS = tuple((dy, dx) for dy in range(N_YH) for dx in range(N_X))[1:]


def dot_nt(left, right):
    return lax.dot_general(left, right, NT, precision=HIGHEST, preferred_element_type=F32)


def dot_nn(left, right):
    return lax.dot_general(left, right, NN, precision=HIGHEST, preferred_element_type=F32)


def matmul(left, right, dims):
    return lax.dot_general(left, right, dims, preferred_element_type=F32)


def halves(values):
    high = values.astype(BF16)
    return high, (values - high.astype(F32)).astype(BF16)


def slots_of(index, groups):
    piece, within = index // 8, index % 8
    return ((piece % 2) * groups + piece // 2) * 8 + within


def onehots(ahead, across, slots, count):
    column = jnp.transpose(jnp.broadcast_to(slots.astype(F32), (TILES, TILES)))
    lane = lax.broadcasted_iota(jnp.int32, (TILES, count), 1).astype(F32)
    ahead[...] = (lane == jnp.concatenate([column, column], axis=1)[:, :count]).astype(F32).astype(BF16)
    across[...] = (lax.broadcasted_iota(jnp.int32, (count, TILES), 0) == slots).astype(F32).astype(BF16)


def pick(picked, pieces, ahead, count):
    for m in range(VECS // 2):
        pair = pieces[:, 16 * m:16 * m + 16, :].astype(F32)
        even = pair[:, 0:8, :].reshape(count, TILE).astype(BF16)
        odd = pair[:, 8:16, :].reshape(count, TILE).astype(BF16)
        chosen = matmul(ahead[...], jnp.concatenate([even, odd], axis=1), NN)
        picked[pl.ds(2 * m, TILES, stride=VECS), :] = chosen[:, :TILE]
        picked[pl.ds(2 * m + 1, TILES, stride=VECS), :] = chosen[:, TILE:]


def place(terms, products, across, count):
    left = jnp.concatenate([across[...], across[...]], axis=1)
    for v in range(0, VECS, 2):
        columns = []
        for u in (v, v + 1):
            columns.append(jnp.concatenate(halves(products[pl.ds(u, TILES, stride=VECS), :]), axis=0))
        total = matmul(left, jnp.concatenate(columns, axis=1), NN)
        terms[:, 8 * v:8 * v + 8, :] = total[:, :TILE].reshape(count // 8, 8, TILE)
        terms[:, 8 * v + 8:8 * v + 16, :] = total[:, TILE:].reshape(count // 8, 8, TILE)


def multiply(products, picked, blocks):
    upper = lax.broadcasted_iota(jnp.int32, (16, TILE), 0) < 8

    def step(i, carry):
        for u in range(32):
            k = (i * 32 + u) * 2
            at = pl.ds(pl.multiple_of(k * 8, 16), 16)
            vectors = picked[at, :]
            left = jnp.concatenate(
                [jnp.where(upper, vectors, 0.0), jnp.where(upper, 0.0, vectors)], axis=1
            ).astype(BF16)
            products[at, :] = matmul(left, blocks[pl.ds(k, 2)].reshape(2 * TILE, TILE), NN)
        return carry

    lax.fori_loop(0, TILES // 64, step, 0)


def with_stack(sums, others, own):
    left, first, second = [], [], []
    for p in range(sums.shape[0]):
        for t in range(8):
            left.append(jnp.concatenate(halves(sums[p, pl.ds(t, VECS, stride=8), :]), axis=0))
            first.append(others[p, 16 * t:16 * t + 16, :])
            second.append(own[p, 8 * t:8 * t + 8, :].astype(BF16))
    left = jnp.concatenate(left, axis=1)
    first = matmul(left, jnp.concatenate(first, axis=1), NT)
    second = matmul(left, jnp.concatenate(second, axis=1), NT)
    both = jnp.concatenate([first, second], axis=1)
    return both[0:8] + both[8:16]


def pack(values):
    line = lax.broadcasted_iota(jnp.int32, (VECS, TILE), 0) % 4
    moved = jnp.where(line == 0, values, 0.0)
    for j in range(1, 4):
        moved = moved + jnp.where(line == j, pltpu.roll(values, 32 * j, axis=1), 0.0)
    return jnp.concatenate(
        [jnp.sum(moved[0:4], axis=0, keepdims=True), jnp.sum(moved[4:8], axis=0, keepdims=True)], axis=0
    )


def unpack(values):
    line = lax.broadcasted_iota(jnp.int32, (VECS, TILE), 0) % 4
    spread = jnp.concatenate(
        [jnp.broadcast_to(values[0:1], (4, TILE)), jnp.broadcast_to(values[1:2], (4, TILE))], axis=0
    )
    moved = jnp.where(line == 0, spread, 0.0)
    for j in range(1, 4):
        moved = moved + jnp.where(line == j, pltpu.roll(spread, TILE - 32 * j, axis=1), 0.0)
    return moved


def tree(terms):
    while len(terms) > 1:
        terms = [a + b for a, b in zip(terms[::2], terms[1::2])] + terms[len(terms) // 2 * 2:]
    return terms[0]


def by_tile(out, pieces, scratch):
    for p in range(out.shape[0]):
        scratch[...] = pieces[p].astype(F32)
        for t in range(8):
            out[p, 8 * t:8 * t + 8, :] = scratch[pl.ds(t, VECS, stride=8), :]


def kernel(
    tiles_hbm, row_hbm, col_hbm, basis_hbm, image_hbm, search_hbm, simage_hbm, ritz_hbm,
    ob, oi, opv,
    tiles, turned, row_v, col_v, ritz_s, work, images, pieces, scratch,
    ahead_r, across_r, ahead_c, across_c, picked, products,
    colbuf, rowbuf, others_c, others_r, own_c, own_r,
    rowterms, colterms, rowlow, ysib, rowsum, zlow, zr, csib, colsum, clow, cr,
    g_core, g_xy, g_yl, g_z, l_row, l_col,
    in_sem,
    cA_s, cA_r, cB_s, cB_r, zA_s, zA_r, yB_s, yB_r,
    oz_s, oz_r, on_s, on_r, oy_s, oy_r, ox_s, ox_r,
    ry_s, ry_r, rz_s, rz_r, sc_s, sc_r, sx_s, sx_r,
    gc_s, gc_r, gx_s, gx_r, gy_s, gy_r, gz_s, gz_r,
    lr_s, lr_r, ll_s, ll_r,
):
    row = lax.axis_index("row")
    col = lax.axis_index("col")
    xy, core = row // 2, row % 2
    yh, x = xy // N_X, xy % N_X
    z, yl = col // 2, col % 2
    sibling = (xy * 2 + 1 - core, col)
    across = (row, z * 2 + 1 - yl)

    def plane(dy, dx):
        return ((yh + dy) % N_YH) * N_X + (x + dx) % N_X

    def z_at(d):
        return (z + d) % N_Z

    def z_peer(d):
        return (row, z_at(d) * 2 + yl)

    def xy_peer(o):
        return (plane(*o) * 2 + core, col)

    def xy_from(o):
        return plane(N_YH - o[0], N_X - o[1])

    barrier = pltpu.get_barrier_semaphore()
    def col_peer(d, e):
        return (row, z_at(d) * 2 + (yl ^ e))

    everyone = [col_peer(d, e) for d, e in IN_COL] + [(row ^ d, col) for d in range(1, N_ROW)]
    for peer in everyone:
        pl.semaphore_signal(barrier, inc=1, device_id=peer, device_id_type=MESH)

    loads = [
        pltpu.make_async_copy(basis_hbm, work.at[pl.ds(0, 8)], in_sem.at[0]),
        pltpu.make_async_copy(image_hbm, work.at[pl.ds(24, 8)], in_sem.at[1]),
        pltpu.make_async_copy(ritz_hbm, ritz_s, in_sem.at[2]),
        pltpu.make_async_copy(search_hbm, work.at[pl.ds(16, 8)], in_sem.at[3]),
        pltpu.make_async_copy(simage_hbm, work.at[pl.ds(32, 8)], in_sem.at[4]),
        pltpu.make_async_copy(row_hbm, row_v, in_sem.at[5]),
        pltpu.make_async_copy(col_hbm, col_v, in_sem.at[6]),
        pltpu.make_async_copy(tiles_hbm.at[0, 0], tiles, in_sem.at[7]),
    ]
    for load in loads:
        load.start()
    for load in loads[:4]:
        load.wait()
    v_index = lax.broadcasted_iota(jnp.int32, (VECS, 1), 0)
    ritz = jnp.zeros((VECS, 1), F32)
    for v in range(VECS):
        ritz = jnp.where(v_index == v, ritz_s[v], ritz)
    residual = work[24:32, :] - ritz * work[0:8, :]
    work[8:16, :] = residual
    mine_col = core * N_XY + xy
    mine_row = yl * N_Z + z
    for t in range(8):
        cut = slice(t * TILE, (t + 1) * TILE)
        pieces[pl.ds(t, VECS, stride=8), :] = residual[:, cut]
        pair = jnp.concatenate([work[0:8, cut], work[16:24, cut]], axis=0).astype(BF16)
        others_c[xy, 16 * t:16 * t + 16, :] = pair
        others_r[z, 16 * t:16 * t + 16, :] = pair
    lowered = pieces[...].astype(BF16)
    colbuf[mine_col] = lowered
    rowbuf[mine_row] = lowered

    pl.semaphore_wait(barrier, len(everyone))

    sends = []

    def remote(src, dst, ss, rs, peer):
        return pltpu.make_async_remote_copy(
            src_ref=src, dst_ref=dst, send_sem=ss, recv_sem=rs, device_id=peer, device_id_type=MESH
        )

    def send(src, dst, ss, rs, peer):
        copy = remote(src, dst, ss, rs, peer)
        copy.start()
        sends.append(copy)

    def arrived(dst, ss, rs, peer):
        remote(dst, dst, ss, rs, peer).wait_recv()

    for d in Z_ORDER:
        send(rowbuf.at[mine_row], rowbuf.at[mine_row], zA_s.at[d], zA_r.at[d], z_peer(d))
    for j, o in enumerate(OFFSETS):
        send(colbuf.at[mine_col], colbuf.at[mine_col], cA_s.at[j], cA_r.at[j], xy_peer(o))
    send(rowbuf.at[mine_row], rowbuf.at[mine_row], yB_s.at[0], yB_r.at[0], across)

    def others_start():
        for d in (6, 3, 9):
            send(others_r.at[z], others_r.at[z], oz_s.at[d], oz_r.at[d], z_peer(d))
        for d in (2, 1, 3):
            send(others_c.at[xy], others_c.at[xy], oy_s.at[d], oy_r.at[d], xy_peer((d, 0)))
        for d in (2, 1, 3):
            send(others_c.at[xy], others_c.at[xy], ox_s.at[0, d], ox_r.at[0, d], xy_peer((0, d)))

    others_start()

    for load in loads[5:7]:
        load.wait()
    onehots(ahead_r, across_r, slots_of(row_v[0], N_Z), N_COL * 8)
    onehots(ahead_c, across_c, slots_of(col_v[0], N_XY), N_ROW * 8)

    loads[4].wait()
    given = dot_nt(work[0:24, :], work[0:40, :])
    g_core[core] = jnp.concatenate(
        [given[0:8], given[8:16], given[16:24], jnp.zeros((8, 8), F32)], axis=1
    )
    send(g_core.at[core], g_core.at[core], gc_s, gc_r, sibling)

    loads[7].wait()

    def turn(i, carry):
        for u in range(16):
            turned[i * 16 + u] = tiles[i * 16 + u].T
        return carry

    lax.fori_loop(0, TILES // 16, turn, 0)

    for dy in range(N_YH):
        for dx in range(N_X):
            if (dy, dx) != (0, 0):
                j = OFFSETS.index((dy, dx))
                arrived(colbuf.at[core * N_XY + xy_from((dy, dx))], cA_s.at[j], cA_r.at[j], xy_peer((dy, dx)))
        block = colbuf.at[pl.ds(core * N_XY + ((yh + N_YH - dy) % N_YH) * N_X, N_X)]
        send(block, block, cB_s.at[dy], cB_r.at[dy], sibling)
    for d in reversed(Z_ORDER):
        here = rowbuf.at[yl * N_Z + z_at(N_Z - d)]
        arrived(here, zA_s.at[d], zA_r.at[d], z_peer(d))
        send(here, here, yB_s.at[d], yB_r.at[d], across)

    def others_on():
        for d in (1, 3, 2):
            here = others_c.at[plane(N_YH - d, 0)]
            arrived(here, oy_s.at[d], oy_r.at[d], xy_peer((d, 0)))
            for e in (2, 1, 3):
                send(here, here, ox_s.at[d, e], ox_r.at[d, e], xy_peer((0, e)))

    others_on()
    for d in (0, 3, 9, 6):
        here = others_r.at[z_at(N_Z - d)]
        if d:
            arrived(here, oz_s.at[d], oz_r.at[d], z_peer(d))
        for e in (1, N_Z - 1):
            send(here, here, on_s.at[e // 2, d // 3], on_r.at[e // 2, d // 3], z_peer(e))

    arrived(g_core.at[1 - core], gc_s, gc_r, sibling)
    g_xy[xy] = g_core[0] + g_core[1]
    for j, o in enumerate(OFFSETS):
        send(g_xy.at[xy], g_xy.at[xy], gx_s.at[j], gx_r.at[j], xy_peer(o))

    for dy in range(N_YH):
        block = colbuf.at[pl.ds((1 - core) * N_XY + ((yh + N_YH - dy) % N_YH) * N_X, N_X)]
        arrived(block, cB_s.at[dy], cB_r.at[dy], sibling)
    pick(picked, colbuf, ahead_c, N_ROW * 8)
    multiply(products, picked, turned)
    place(rowterms, products, across_r, N_COL * 8)
    for q in range(2):
        half = pl.ds(q * N_Z // 2, N_Z // 2)
        rowlow[half] = rowterms[pl.ds((1 - yl) * N_Z + q * N_Z // 2, N_Z // 2)].astype(BF16)
        send(rowlow.at[half], ysib.at[half], ry_s.at[q], ry_r.at[q], across)

    for d in range(N_Z):
        arrived(rowbuf.at[(1 - yl) * N_Z + z_at(N_Z - d)], yB_s.at[d], yB_r.at[d], across)
    pick(picked, rowbuf, ahead_r, N_COL * 8)
    multiply(products, picked, tiles)
    place(colterms, products, across_c, N_ROW * 8)
    chunk = N_XY // 4
    for q in range(4):
        send(
            colterms.at[pl.ds((1 - core) * N_XY + q * chunk, chunk)],
            csib.at[pl.ds(q * chunk, chunk)], sc_s.at[q], sc_r.at[q], sibling,
        )

    for j, o in enumerate(OFFSETS):
        arrived(g_xy.at[xy_from(o)], gx_s.at[j], gx_r.at[j], xy_peer(o))
    total = g_xy[0]
    for j in range(1, N_XY):
        total = total + g_xy[j]
    g_yl[yl] = total
    send(g_yl.at[yl], g_yl.at[yl], gy_s, gy_r, across)
    by_tile(own_c, colbuf.at[pl.ds(core * N_XY, N_XY)], scratch)
    by_tile(own_r, rowbuf.at[pl.ds(yl * N_Z, N_Z)], scratch)

    for q in range(4):
        at = pl.ds(q * chunk, chunk)
        arrived(csib.at[at], sc_s.at[q], sc_r.at[q], sibling)
        both = colterms[pl.ds(core * N_XY + q * chunk, chunk)] + csib[at]
        colsum[at] = both
        clow[at] = both.astype(BF16)
    for j, o in enumerate(OFFSETS):
        send(clow.at[plane(*o)], cr.at[xy], sx_s.at[j], sx_r.at[j], xy_peer(o))
    arrived(g_yl.at[1 - yl], gy_s, gy_r, across)
    g_z[z] = g_yl[0] + g_yl[1]
    for d in Z_ORDER:
        send(g_z.at[z], g_z.at[z], gz_s.at[d], gz_r.at[d], z_peer(d))
    for q in range(2):
        half = pl.ds(q * N_Z // 2, N_Z // 2)
        arrived(ysib.at[half], ry_s.at[q], ry_r.at[q], across)
        both = rowterms[pl.ds(yl * N_Z + q * N_Z // 2, N_Z // 2)] + ysib[half].astype(F32)
        rowsum[half] = both
        zlow[half] = both.astype(BF16)
    for d in Z_ORDER:
        send(zlow.at[z_at(d)], zr.at[z], rz_s.at[d], rz_r.at[d], z_peer(d))
    for d in (1, 2, 3):
        for e in range(N_YH):
            arrived(others_c.at[plane(N_YH - e, N_X - d)], ox_s.at[e, d], ox_r.at[e, d], xy_peer((0, d)))
    in_plane = with_stack(colsum, others_c, own_c)
    for d in (0, 3, 9, 6):
        for e in (1, N_Z - 1):
            arrived(others_r.at[z_at(2 * N_Z - d - e)], on_s.at[e // 2, d // 3], on_r.at[e // 2, d // 3], z_peer(e))
    last = in_plane + with_stack(rowsum, others_r, own_r)
    l_row[row] = pack(jnp.concatenate([last, jnp.zeros((VECS, TILE - 24), F32)], axis=1))
    for d in range(1, N_ROW):
        send(l_row.at[row], l_row.at[row], lr_s.at[d], lr_r.at[d], (row ^ d, col))

    for d in range(1, N_ROW):
        arrived(l_row.at[row ^ d], lr_s.at[d], lr_r.at[d], (row ^ d, col))
    l_col[col] = tree([l_row[j] for j in range(N_ROW)])
    for d, e in IN_COL:
        send(l_col.at[col], l_col.at[col], ll_s.at[d, e], ll_r.at[d, e], col_peer(d, e))

    for d in Z_ORDER:
        arrived(g_z.at[z_at(N_Z - d)], gz_s.at[d], gz_r.at[d], z_peer(d))
    total = g_z[0]
    for j in range(1, N_Z):
        total = total + g_z[j]
    n_total = F32(1024 * N_ROW * N_COL)
    total = total / n_total
    total = jnp.concatenate([total[:, 0:40], total[:, 40:80], total[:, 80:120]], axis=0)
    rows = lax.broadcasted_iota(jnp.int32, (24, 24), 0)
    columns = lax.broadcasted_iota(jnp.int32, (24, 24), 1)
    matrix = jnp.concatenate([total[:, 0:24], jnp.where(rows == columns, F32(1.0), F32(0.0))], axis=1)
    index = lax.broadcasted_iota(jnp.int32, (24, 1), 0)
    for step in range(24):
        pivot = jnp.sqrt(matrix[step:step + 1, step:step + 1])
        scaled = matrix[step:step + 1, :] / pivot
        factor = matrix[:, step:step + 1] / pivot
        matrix = jnp.where(
            index == step, scaled, jnp.where(index > step, matrix - factor * scaled, matrix)
        )
    inverse = matrix[:, 24:48]
    reordered = jnp.concatenate([inverse[:, 0:8], inverse[:, 16:24], inverse[:, 8:16]], axis=1)
    given = dot_nt(dot_nn(inverse, total[:, 24:32]), inverse[:, 0:8]) + dot_nt(
        dot_nn(inverse, total[:, 32:40]), inverse[:, 16:24]
    )
    ob[...] = dot_nn(inverse, work[0:24, :])

    image = rowsum[z] + colsum[xy]
    for d in reversed(Z_ORDER):
        arrived(zr.at[z_at(N_Z - d)], rz_s.at[d], rz_r.at[d], z_peer(d))
        image = image + zr[z_at(N_Z - d)].astype(F32)
    for j, o in enumerate(OFFSETS):
        arrived(cr.at[xy_from(o)], sx_s.at[j], sx_r.at[j], xy_peer(o))
        image = image + cr[xy_from(o)].astype(F32)
    pieces[...] = image
    for t in range(8):
        images[8:16, t * TILE:(t + 1) * TILE] = pieces[pl.ds(t, VECS, stride=8), :]
    images[0:8, :] = work[24:32, :]
    images[16:24, :] = work[32:40, :]
    oi[...] = dot_nn(inverse, images[...])

    for d, e in IN_COL:
        arrived(l_col.at[z_at(N_Z - d) * 2 + (yl ^ e)], ll_s.at[d, e], ll_r.at[d, e], col_peer(d, e))
    late = unpack(tree([l_col[j] for j in range(N_COL)])) / n_total
    opv[...] = given + dot_nt(dot_nt(reordered, late[:, 0:24]), inverse[:, 8:16])
    for copy in sends:
        copy.wait_send()


def on_device(tiles, tile_row, tile_col, basis, basis_image, search, search_image, ritz_values):
    vmem, dma = pltpu.VMEM, pltpu.SemaphoreType.DMA
    n_off = N_XY - 1
    outs = (
        jax.ShapeDtypeStruct((24, 1024), F32),
        jax.ShapeDtypeStruct((24, 1024), F32),
        jax.ShapeDtypeStruct((24, 24), F32),
    )

    def pairs(*shapes):
        return [dma(shape) for shape in shapes for _ in range(2)]

    results = pl.pallas_call(
        kernel,
        out_shape=tuple(vmem(out.shape, F32) for out in outs),
        in_specs=[pl.BlockSpec(memory_space=pl.ANY)] * 8,
        out_specs=[pl.BlockSpec(memory_space=vmem)] * 3,
        scratch_shapes=[
            vmem((TILES, TILE, TILE), BF16),
            vmem((TILES, TILE, TILE), BF16),
            vmem((1, 1, TILES), jnp.int32),
            vmem((1, 1, TILES), jnp.int32),
            pltpu.SMEM((VECS,), F32),
            vmem((40, 1024), F32),
            vmem((24, 1024), F32),
            vmem((64, TILE), F32),
            vmem((64, TILE), F32),
            vmem((TILES, N_COL * 8), BF16),
            vmem((N_COL * 8, TILES), BF16),
            vmem((TILES, N_ROW * 8), BF16),
            vmem((N_ROW * 8, TILES), BF16),
            vmem((TILES * VECS, TILE), F32),
            vmem((TILES * VECS, TILE), F32),
            vmem((N_ROW, 64, TILE), BF16),
            vmem((N_COL, 64, TILE), BF16),
            vmem((N_XY, 128, TILE), BF16),
            vmem((N_Z, 128, TILE), BF16),
            vmem((N_XY, 64, TILE), F32),
            vmem((N_Z, 64, TILE), F32),
            vmem((N_COL, 64, TILE), F32),
            vmem((N_ROW, 64, TILE), F32),
            vmem((N_Z, 64, TILE), BF16),
            vmem((N_Z, 64, TILE), BF16),
            vmem((N_Z, 64, TILE), F32),
            vmem((N_Z, 64, TILE), BF16),
            vmem((N_Z, 64, TILE), BF16),
            vmem((N_XY, 64, TILE), F32),
            vmem((N_XY, 64, TILE), F32),
            vmem((N_XY, 64, TILE), BF16),
            vmem((N_XY, 64, TILE), BF16),
            vmem((2, 8, TILE), F32),
            vmem((N_XY, 8, TILE), F32),
            vmem((2, 8, TILE), F32),
            vmem((N_Z, 8, TILE), F32),
            vmem((N_ROW, 2, TILE), F32),
            vmem((N_COL, 2, TILE), F32),
            dma((8,)),
        ] + pairs(
            (n_off,), (N_YH,), (N_Z,), (N_Z,), (N_Z,), (6, 4), (N_YH,), (N_YH, N_X),
            (2,), (N_Z,), (4,), (n_off,),
            (), (n_off,), (), (N_Z,), (N_ROW,), (N_Z, 2),
        ),
        compiler_params=pltpu.CompilerParams(
            collective_id=0, has_side_effects=True, vmem_limit_bytes=56 * 2**20
        ),
        name="step",
    )(tiles, tile_row, tile_col, basis, basis_image, search, search_image, ritz_values)
    return tuple(results)


def solution(mesh):
    vectors = P(None, ("row", "col"))
    return jax.shard_map(
        on_device,
        mesh=mesh,
        in_specs=(
            P("row", "col", None, None, None),
            P("row", "col", None),
            P("row", "col", None),
            vectors, vectors, vectors, vectors,
            P(),
        ),
        out_specs=(vectors, vectors, P()),
        check_vma=False,
    )
```

```python
import jax
import jax.numpy as jnp
from jax import lax
from jax.experimental import pallas as pl
from jax.experimental.pallas import tpu as pltpu
from jax.sharding import PartitionSpec as P

MESH = pl.DeviceIdType.MESH
TILE = 128
VECS = 8
TILES = 128
N_YH, N_X, N_Z = 4, 4, 12
N_XY = N_YH * N_X
N_ROW, N_COL = 2 * N_XY, 2 * N_Z
F32 = jnp.float32
BF16 = jnp.bfloat16
HIGHEST = lax.Precision.HIGHEST
NT = (((1,), (1,)), ((), ()))
NN = (((1,), (0,)), ((), ()))
Z_ORDER = (6, 5, 7, 4, 8, 3, 9, 2, 10, 1, 11)
IN_COL = tuple((d, e) for d in Z_ORDER for e in (0, 1)) + ((0, 1),)
OFFSETS = tuple((dy, dx) for dy in range(N_YH) for dx in range(N_X))[1:]


def dot_nt(left, right):
    return lax.dot_general(left, right, NT, precision=HIGHEST, preferred_element_type=F32)


def dot_nn(left, right):
    return lax.dot_general(left, right, NN, precision=HIGHEST, preferred_element_type=F32)


def matmul(left, right, dims):
    return lax.dot_general(left, right, dims, preferred_element_type=F32)


def halves(values):
    high = values.astype(BF16)
    return high, (values - high.astype(F32)).astype(BF16)


def slots_of(index, groups):
    piece, within = index // 8, index % 8
    return ((piece % 2) * groups + piece // 2) * 8 + within


def onehots(ahead, across, slots, count):
    column = jnp.transpose(jnp.broadcast_to(slots.astype(F32), (TILES, TILES)))
    lane = lax.broadcasted_iota(jnp.int32, (TILES, count), 1).astype(F32)
    ahead[...] = (lane == jnp.concatenate([column, column], axis=1)[:, :count]).astype(F32).astype(BF16)
    across[...] = (lax.broadcasted_iota(jnp.int32, (count, TILES), 0) == slots).astype(F32).astype(BF16)


def pick(picked, pieces, ahead, count):
    for m in range(VECS // 2):
        pair = pieces[:, 16 * m:16 * m + 16, :].astype(F32)
        even = pair[:, 0:8, :].reshape(count, TILE).astype(BF16)
        odd = pair[:, 8:16, :].reshape(count, TILE).astype(BF16)
        chosen = matmul(ahead[...], jnp.concatenate([even, odd], axis=1), NN)
        picked[pl.ds(2 * m, TILES, stride=VECS), :] = chosen[:, :TILE]
        picked[pl.ds(2 * m + 1, TILES, stride=VECS), :] = chosen[:, TILE:]


def place(terms, products, across, count):
    left = jnp.concatenate([across[...], across[...]], axis=1)
    for v in range(0, VECS, 2):
        columns = []
        for u in (v, v + 1):
            columns.append(jnp.concatenate(halves(products[pl.ds(u, TILES, stride=VECS), :]), axis=0))
        total = matmul(left, jnp.concatenate(columns, axis=1), NN)
        terms[:, 8 * v:8 * v + 8, :] = total[:, :TILE].reshape(count // 8, 8, TILE)
        terms[:, 8 * v + 8:8 * v + 16, :] = total[:, TILE:].reshape(count // 8, 8, TILE)


def multiply(products, picked, blocks):
    upper = lax.broadcasted_iota(jnp.int32, (16, TILE), 0) < 8

    def step(i, carry):
        for u in range(32):
            k = (i * 32 + u) * 2
            at = pl.ds(pl.multiple_of(k * 8, 16), 16)
            vectors = picked[at, :]
            left = jnp.concatenate(
                [jnp.where(upper, vectors, 0.0), jnp.where(upper, 0.0, vectors)], axis=1
            ).astype(BF16)
            products[at, :] = matmul(left, blocks[pl.ds(k, 2)].reshape(2 * TILE, TILE), NN)
        return carry

    lax.fori_loop(0, TILES // 64, step, 0)


def with_stack(sums, others, own):
    left, first, second = [], [], []
    for p in range(sums.shape[0]):
        for t in range(8):
            left.append(jnp.concatenate(halves(sums[p, pl.ds(t, VECS, stride=8), :]), axis=0))
            first.append(others[p, 16 * t:16 * t + 16, :])
            second.append(own[p, 8 * t:8 * t + 8, :].astype(BF16))
    left = jnp.concatenate(left, axis=1)
    first = matmul(left, jnp.concatenate(first, axis=1), NT)
    second = matmul(left, jnp.concatenate(second, axis=1), NT)
    both = jnp.concatenate([first, second], axis=1)
    return both[0:8] + both[8:16]


def pack(values):
    line = lax.broadcasted_iota(jnp.int32, (VECS, TILE), 0) % 4
    moved = jnp.where(line == 0, values, 0.0)
    for j in range(1, 4):
        moved = moved + jnp.where(line == j, pltpu.roll(values, 32 * j, axis=1), 0.0)
    return jnp.concatenate(
        [jnp.sum(moved[0:4], axis=0, keepdims=True), jnp.sum(moved[4:8], axis=0, keepdims=True)], axis=0
    )


def unpack(values):
    line = lax.broadcasted_iota(jnp.int32, (VECS, TILE), 0) % 4
    spread = jnp.concatenate(
        [jnp.broadcast_to(values[0:1], (4, TILE)), jnp.broadcast_to(values[1:2], (4, TILE))], axis=0
    )
    moved = jnp.where(line == 0, spread, 0.0)
    for j in range(1, 4):
        moved = moved + jnp.where(line == j, pltpu.roll(spread, TILE - 32 * j, axis=1), 0.0)
    return moved


def tree(terms):
    while len(terms) > 1:
        terms = [a + b for a, b in zip(terms[::2], terms[1::2])] + terms[len(terms) // 2 * 2:]
    return terms[0]


def by_tile(out, pieces, scratch):
    for p in range(out.shape[0]):
        scratch[...] = pieces[p].astype(F32)
        for t in range(8):
            out[p, 8 * t:8 * t + 8, :] = scratch[pl.ds(t, VECS, stride=8), :]


def kernel(
    tiles_hbm, row_hbm, col_hbm, basis_hbm, image_hbm, search_hbm, simage_hbm, ritz_hbm,
    ob, oi, opv,
    tiles, turned, row_v, col_v, ritz_s, work, images, pieces, scratch,
    ahead_r, across_r, ahead_c, across_c, picked, products,
    colbuf, rowbuf, others_c, others_r, own_c, own_r,
    rowterms, colterms, rowlow, ysib, rowsum, zlow, zr, csib, colsum, clow, cr,
    g_core, g_xy, g_yl, g_z, l_row, l_col,
    in_sem,
    cA_s, cA_r, cB_s, cB_r, zA_s, zA_r, yB_s, yB_r,
    oz_s, oz_r, on_s, on_r, oy_s, oy_r, ox_s, ox_r,
    ry_s, ry_r, rz_s, rz_r, sc_s, sc_r, sx_s, sx_r,
    gc_s, gc_r, gx_s, gx_r, gy_s, gy_r, gz_s, gz_r,
    lr_s, lr_r, ll_s, ll_r,
):
    row = lax.axis_index("row")
    col = lax.axis_index("col")
    xy, core = row // 2, row % 2
    yh, x = xy // N_X, xy % N_X
    z, yl = col // 2, col % 2
    sibling = (xy * 2 + 1 - core, col)
    across = (row, z * 2 + 1 - yl)

    def plane(dy, dx):
        return ((yh + dy) % N_YH) * N_X + (x + dx) % N_X

    def z_at(d):
        return (z + d) % N_Z

    def z_peer(d):
        return (row, z_at(d) * 2 + yl)

    def xy_peer(o):
        return (plane(*o) * 2 + core, col)

    def xy_from(o):
        return plane(N_YH - o[0], N_X - o[1])

    barrier = pltpu.get_barrier_semaphore()
    def col_peer(d, e):
        return (row, z_at(d) * 2 + (yl ^ e))

    everyone = [col_peer(d, e) for d, e in IN_COL] + [(row ^ d, col) for d in range(1, N_ROW)]
    for peer in everyone:
        pl.semaphore_signal(barrier, inc=1, device_id=peer, device_id_type=MESH)

    loads = [
        pltpu.make_async_copy(basis_hbm, work.at[pl.ds(0, 8)], in_sem.at[0]),
        pltpu.make_async_copy(image_hbm, work.at[pl.ds(24, 8)], in_sem.at[1]),
        pltpu.make_async_copy(ritz_hbm, ritz_s, in_sem.at[2]),
        pltpu.make_async_copy(search_hbm, work.at[pl.ds(16, 8)], in_sem.at[3]),
        pltpu.make_async_copy(simage_hbm, work.at[pl.ds(32, 8)], in_sem.at[4]),
        pltpu.make_async_copy(row_hbm, row_v, in_sem.at[5]),
        pltpu.make_async_copy(col_hbm, col_v, in_sem.at[6]),
        pltpu.make_async_copy(tiles_hbm.at[0, 0], tiles, in_sem.at[7]),
    ]
    for load in loads:
        load.start()
    for load in loads[:4]:
        load.wait()
    v_index = lax.broadcasted_iota(jnp.int32, (VECS, 1), 0)
    ritz = jnp.zeros((VECS, 1), F32)
    for v in range(VECS):
        ritz = jnp.where(v_index == v, ritz_s[v], ritz)
    residual = work[24:32, :] - ritz * work[0:8, :]
    work[8:16, :] = residual
    mine_col = core * N_XY + xy
    mine_row = yl * N_Z + z
    for t in range(8):
        cut = slice(t * TILE, (t + 1) * TILE)
        pieces[pl.ds(t, VECS, stride=8), :] = residual[:, cut]
        pair = jnp.concatenate([work[0:8, cut], work[16:24, cut]], axis=0).astype(BF16)
        others_c[xy, 16 * t:16 * t + 16, :] = pair
        others_r[z, 16 * t:16 * t + 16, :] = pair
    lowered = pieces[...].astype(BF16)
    colbuf[mine_col] = lowered
    rowbuf[mine_row] = lowered

    pl.semaphore_wait(barrier, len(everyone))

    sends = []

    def remote(src, dst, ss, rs, peer):
        return pltpu.make_async_remote_copy(
            src_ref=src, dst_ref=dst, send_sem=ss, recv_sem=rs, device_id=peer, device_id_type=MESH
        )

    def send(src, dst, ss, rs, peer):
        copy = remote(src, dst, ss, rs, peer)
        copy.start()
        sends.append(copy)

    def arrived(dst, ss, rs, peer):
        remote(dst, dst, ss, rs, peer).wait_recv()

    for d in Z_ORDER:
        send(rowbuf.at[mine_row], rowbuf.at[mine_row], zA_s.at[d], zA_r.at[d], z_peer(d))
    for j, o in enumerate(OFFSETS):
        send(colbuf.at[mine_col], colbuf.at[mine_col], cA_s.at[j], cA_r.at[j], xy_peer(o))
    send(rowbuf.at[mine_row], rowbuf.at[mine_row], yB_s.at[0], yB_r.at[0], across)

    def others_start():
        for d in (6, 3, 9):
            send(others_r.at[z], others_r.at[z], oz_s.at[d], oz_r.at[d], z_peer(d))
        for d in (2, 1, 3):
            send(others_c.at[xy], others_c.at[xy], oy_s.at[d], oy_r.at[d], xy_peer((d, 0)))
        for d in (2, 1, 3):
            send(others_c.at[xy], others_c.at[xy], ox_s.at[0, d], ox_r.at[0, d], xy_peer((0, d)))

    others_start()

    for load in loads[5:7]:
        load.wait()
    onehots(ahead_r, across_r, slots_of(row_v[0], N_Z), N_COL * 8)
    onehots(ahead_c, across_c, slots_of(col_v[0], N_XY), N_ROW * 8)

    loads[4].wait()
    given = dot_nt(work[0:24, :], work[0:40, :])
    g_core[core] = jnp.concatenate(
        [given[0:8], given[8:16], given[16:24], jnp.zeros((8, 8), F32)], axis=1
    )
    send(g_core.at[core], g_core.at[core], gc_s, gc_r, sibling)

    loads[7].wait()

    def turn(i, carry):
        for u in range(16):
            turned[i * 16 + u] = tiles[i * 16 + u].T
        return carry

    lax.fori_loop(0, TILES // 16, turn, 0)

    for dy in range(N_YH):
        for dx in range(N_X):
            if (dy, dx) != (0, 0):
                j = OFFSETS.index((dy, dx))
                arrived(colbuf.at[core * N_XY + xy_from((dy, dx))], cA_s.at[j], cA_r.at[j], xy_peer((dy, dx)))
        block = colbuf.at[pl.ds(core * N_XY + ((yh + N_YH - dy) % N_YH) * N_X, N_X)]
        send(block, block, cB_s.at[dy], cB_r.at[dy], sibling)
    for d in reversed(Z_ORDER):
        here = rowbuf.at[yl * N_Z + z_at(N_Z - d)]
        arrived(here, zA_s.at[d], zA_r.at[d], z_peer(d))
        send(here, here, yB_s.at[d], yB_r.at[d], across)

    def others_on():
        for d in (1, 3, 2):
            here = others_c.at[plane(N_YH - d, 0)]
            arrived(here, oy_s.at[d], oy_r.at[d], xy_peer((d, 0)))
            for e in (2, 1, 3):
                send(here, here, ox_s.at[d, e], ox_r.at[d, e], xy_peer((0, e)))

    others_on()
    for d in (0, 3, 9, 6):
        here = others_r.at[z_at(N_Z - d)]
        if d:
            arrived(here, oz_s.at[d], oz_r.at[d], z_peer(d))
        for e in (1, N_Z - 1):
            send(here, here, on_s.at[e // 2, d // 3], on_r.at[e // 2, d // 3], z_peer(e))

    arrived(g_core.at[1 - core], gc_s, gc_r, sibling)
    g_xy[xy] = g_core[0] + g_core[1]
    for j, o in enumerate(OFFSETS):
        send(g_xy.at[xy], g_xy.at[xy], gx_s.at[j], gx_r.at[j], xy_peer(o))

    for dy in range(N_YH):
        block = colbuf.at[pl.ds((1 - core) * N_XY + ((yh + N_YH - dy) % N_YH) * N_X, N_X)]
        arrived(block, cB_s.at[dy], cB_r.at[dy], sibling)
    pick(picked, colbuf, ahead_c, N_ROW * 8)
    multiply(products, picked, turned)
    place(rowterms, products, across_r, N_COL * 8)
    for q in range(2):
        half = pl.ds(q * N_Z // 2, N_Z // 2)
        rowlow[half] = rowterms[pl.ds((1 - yl) * N_Z + q * N_Z // 2, N_Z // 2)].astype(BF16)
        send(rowlow.at[half], ysib.at[half], ry_s.at[q], ry_r.at[q], across)

    for d in range(N_Z):
        arrived(rowbuf.at[(1 - yl) * N_Z + z_at(N_Z - d)], yB_s.at[d], yB_r.at[d], across)
    pick(picked, rowbuf, ahead_r, N_COL * 8)
    multiply(products, picked, tiles)
    place(colterms, products, across_c, N_ROW * 8)
    chunk = N_XY // 4
    for q in range(4):
        send(
            colterms.at[pl.ds((1 - core) * N_XY + q * chunk, chunk)],
            csib.at[pl.ds(q * chunk, chunk)], sc_s.at[q], sc_r.at[q], sibling,
        )

    by_tile(own_c, colbuf.at[pl.ds(core * N_XY, N_XY)], scratch)
    by_tile(own_r, rowbuf.at[pl.ds(yl * N_Z, N_Z)], scratch)

    for q in range(4):
        at = pl.ds(q * chunk, chunk)
        arrived(csib.at[at], sc_s.at[q], sc_r.at[q], sibling)
        both = colterms[pl.ds(core * N_XY + q * chunk, chunk)] + csib[at]
        colsum[at] = both
        clow[at] = both.astype(BF16)
    for j, o in enumerate(OFFSETS):
        send(clow.at[plane(*o)], cr.at[xy], sx_s.at[j], sx_r.at[j], xy_peer(o))
    for q in range(2):
        half = pl.ds(q * N_Z // 2, N_Z // 2)
        arrived(ysib.at[half], ry_s.at[q], ry_r.at[q], across)
        both = rowterms[pl.ds(yl * N_Z + q * N_Z // 2, N_Z // 2)] + ysib[half].astype(F32)
        rowsum[half] = both
        zlow[half] = both.astype(BF16)
    for d in Z_ORDER:
        send(zlow.at[z_at(d)], zr.at[z], rz_s.at[d], rz_r.at[d], z_peer(d))
    for j, o in enumerate(OFFSETS):
        arrived(g_xy.at[xy_from(o)], gx_s.at[j], gx_r.at[j], xy_peer(o))
    total = g_xy[0]
    for j in range(1, N_XY):
        total = total + g_xy[j]
    g_yl[yl] = total
    send(g_yl.at[yl], g_yl.at[yl], gy_s, gy_r, across)
    for d in (1, 2, 3):
        for e in range(N_YH):
            arrived(others_c.at[plane(N_YH - e, N_X - d)], ox_s.at[e, d], ox_r.at[e, d], xy_peer((0, d)))
    in_plane = with_stack(colsum, others_c, own_c)
    for d in (0, 3, 9, 6):
        for e in (1, N_Z - 1):
            arrived(others_r.at[z_at(2 * N_Z - d - e)], on_s.at[e // 2, d // 3], on_r.at[e // 2, d // 3], z_peer(e))
    last = in_plane + with_stack(rowsum, others_r, own_r)
    l_row[row] = pack(jnp.concatenate([last, jnp.zeros((VECS, TILE - 24), F32)], axis=1))
    for d in range(1, N_ROW):
        send(l_row.at[row], l_row.at[row], lr_s.at[d], lr_r.at[d], (row ^ d, col))

    arrived(g_yl.at[1 - yl], gy_s, gy_r, across)
    g_z[z] = g_yl[0] + g_yl[1]
    for d in Z_ORDER:
        send(g_z.at[z], g_z.at[z], gz_s.at[d], gz_r.at[d], z_peer(d))
    for d in range(1, N_ROW):
        arrived(l_row.at[row ^ d], lr_s.at[d], lr_r.at[d], (row ^ d, col))
    l_col[col] = tree([l_row[j] for j in range(N_ROW)])
    for d, e in IN_COL:
        send(l_col.at[col], l_col.at[col], ll_s.at[d, e], ll_r.at[d, e], col_peer(d, e))

    for d in Z_ORDER:
        arrived(g_z.at[z_at(N_Z - d)], gz_s.at[d], gz_r.at[d], z_peer(d))
    total = g_z[0]
    for j in range(1, N_Z):
        total = total + g_z[j]
    n_total = F32(1024 * N_ROW * N_COL)
    total = total / n_total
    total = jnp.concatenate([total[:, 0:40], total[:, 40:80], total[:, 80:120]], axis=0)
    rows = lax.broadcasted_iota(jnp.int32, (24, 24), 0)
    columns = lax.broadcasted_iota(jnp.int32, (24, 24), 1)
    matrix = jnp.concatenate([total[:, 0:24], jnp.where(rows == columns, F32(1.0), F32(0.0))], axis=1)
    index = lax.broadcasted_iota(jnp.int32, (24, 1), 0)
    for step in range(24):
        pivot = jnp.sqrt(matrix[step:step + 1, step:step + 1])
        scaled = matrix[step:step + 1, :] / pivot
        factor = matrix[:, step:step + 1] / pivot
        matrix = jnp.where(
            index == step, scaled, jnp.where(index > step, matrix - factor * scaled, matrix)
        )
    inverse = matrix[:, 24:48]
    reordered = jnp.concatenate([inverse[:, 0:8], inverse[:, 16:24], inverse[:, 8:16]], axis=1)
    given = dot_nt(dot_nn(inverse, total[:, 24:32]), inverse[:, 0:8]) + dot_nt(
        dot_nn(inverse, total[:, 32:40]), inverse[:, 16:24]
    )
    ob[...] = dot_nn(inverse, work[0:24, :])

    image = rowsum[z] + colsum[xy]
    for d in reversed(Z_ORDER):
        arrived(zr.at[z_at(N_Z - d)], rz_s.at[d], rz_r.at[d], z_peer(d))
        image = image + zr[z_at(N_Z - d)].astype(F32)
    for j, o in enumerate(OFFSETS):
        arrived(cr.at[xy_from(o)], sx_s.at[j], sx_r.at[j], xy_peer(o))
        image = image + cr[xy_from(o)].astype(F32)
    pieces[...] = image
    for t in range(8):
        images[8:16, t * TILE:(t + 1) * TILE] = pieces[pl.ds(t, VECS, stride=8), :]
    images[0:8, :] = work[24:32, :]
    images[16:24, :] = work[32:40, :]
    oi[...] = dot_nn(inverse, images[...])

    for d, e in IN_COL:
        arrived(l_col.at[z_at(N_Z - d) * 2 + (yl ^ e)], ll_s.at[d, e], ll_r.at[d, e], col_peer(d, e))
    late = unpack(tree([l_col[j] for j in range(N_COL)])) / n_total
    opv[...] = given + dot_nt(dot_nt(reordered, late[:, 0:24]), inverse[:, 8:16])
    for copy in sends:
        copy.wait_send()


def on_device(tiles, tile_row, tile_col, basis, basis_image, search, search_image, ritz_values):
    vmem, dma = pltpu.VMEM, pltpu.SemaphoreType.DMA
    n_off = N_XY - 1
    outs = (
        jax.ShapeDtypeStruct((24, 1024), F32),
        jax.ShapeDtypeStruct((24, 1024), F32),
        jax.ShapeDtypeStruct((24, 24), F32),
    )

    def pairs(*shapes):
        return [dma(shape) for shape in shapes for _ in range(2)]

    results = pl.pallas_call(
        kernel,
        out_shape=tuple(vmem(out.shape, F32) for out in outs),
        in_specs=[pl.BlockSpec(memory_space=pl.ANY)] * 8,
        out_specs=[pl.BlockSpec(memory_space=vmem)] * 3,
        scratch_shapes=[
            vmem((TILES, TILE, TILE), BF16),
            vmem((TILES, TILE, TILE), BF16),
            vmem((1, 1, TILES), jnp.int32),
            vmem((1, 1, TILES), jnp.int32),
            pltpu.SMEM((VECS,), F32),
            vmem((40, 1024), F32),
            vmem((24, 1024), F32),
            vmem((64, TILE), F32),
            vmem((64, TILE), F32),
            vmem((TILES, N_COL * 8), BF16),
            vmem((N_COL * 8, TILES), BF16),
            vmem((TILES, N_ROW * 8), BF16),
            vmem((N_ROW * 8, TILES), BF16),
            vmem((TILES * VECS, TILE), F32),
            vmem((TILES * VECS, TILE), F32),
            vmem((N_ROW, 64, TILE), BF16),
            vmem((N_COL, 64, TILE), BF16),
            vmem((N_XY, 128, TILE), BF16),
            vmem((N_Z, 128, TILE), BF16),
            vmem((N_XY, 64, TILE), F32),
            vmem((N_Z, 64, TILE), F32),
            vmem((N_COL, 64, TILE), F32),
            vmem((N_ROW, 64, TILE), F32),
            vmem((N_Z, 64, TILE), BF16),
            vmem((N_Z, 64, TILE), BF16),
            vmem((N_Z, 64, TILE), F32),
            vmem((N_Z, 64, TILE), BF16),
            vmem((N_Z, 64, TILE), BF16),
            vmem((N_XY, 64, TILE), F32),
            vmem((N_XY, 64, TILE), F32),
            vmem((N_XY, 64, TILE), BF16),
            vmem((N_XY, 64, TILE), BF16),
            vmem((2, 8, TILE), F32),
            vmem((N_XY, 8, TILE), F32),
            vmem((2, 8, TILE), F32),
            vmem((N_Z, 8, TILE), F32),
            vmem((N_ROW, 2, TILE), F32),
            vmem((N_COL, 2, TILE), F32),
            dma((8,)),
        ] + pairs(
            (n_off,), (N_YH,), (N_Z,), (N_Z,), (N_Z,), (6, 4), (N_YH,), (N_YH, N_X),
            (2,), (N_Z,), (4,), (n_off,),
            (), (n_off,), (), (N_Z,), (N_ROW,), (N_Z, 2),
        ),
        compiler_params=pltpu.CompilerParams(
            collective_id=0, has_side_effects=True, vmem_limit_bytes=56 * 2**20
        ),
        name="step",
    )(tiles, tile_row, tile_col, basis, basis_image, search, search_image, ritz_values)
    return tuple(results)


def solution(mesh):
    vectors = P(None, ("row", "col"))
    return jax.shard_map(
        on_device,
        mesh=mesh,
        in_specs=(
            P("row", "col", None, None, None),
            P("row", "col", None),
            P("row", "col", None),
            vectors, vectors, vectors, vectors,
            P(),
        ),
        out_specs=(vectors, vectors, P()),
        check_vma=False,
    )
```

```python
import jax
import jax.numpy as jnp
from jax import lax
from jax.experimental import pallas as pl
from jax.experimental.pallas import tpu as pltpu
from jax.sharding import PartitionSpec as P

MESH = pl.DeviceIdType.MESH
TILE = 128
VECS = 8
TILES = 128
N_YH, N_X, N_Z = 4, 4, 12
N_XY = N_YH * N_X
N_ROW, N_COL = 2 * N_XY, 2 * N_Z
F32 = jnp.float32
BF16 = jnp.bfloat16
HIGHEST = lax.Precision.HIGHEST
NT = (((1,), (1,)), ((), ()))
NN = (((1,), (0,)), ((), ()))
Z_ORDER = (6, 5, 7, 4, 8, 3, 9, 2, 10, 1, 11)
IN_COL = tuple((d, e) for d in Z_ORDER for e in (0, 1)) + ((0, 1),)
OFFSETS = tuple((dy, dx) for dy in range(N_YH) for dx in range(N_X))[1:]


def dot_nt(left, right):
    return lax.dot_general(left, right, NT, precision=HIGHEST, preferred_element_type=F32)


def dot_nn(left, right):
    return lax.dot_general(left, right, NN, precision=HIGHEST, preferred_element_type=F32)


def matmul(left, right, dims):
    return lax.dot_general(left, right, dims, preferred_element_type=F32)


def halves(values):
    high = values.astype(BF16)
    return high, (values - high.astype(F32)).astype(BF16)


def slots_of(index, groups):
    piece, within = index // 8, index % 8
    return ((piece % 2) * groups + piece // 2) * 8 + within


def onehots(ahead, across, slots, count):
    column = jnp.transpose(jnp.broadcast_to(slots.astype(F32), (TILES, TILES)))
    lane = lax.broadcasted_iota(jnp.int32, (TILES, count), 1).astype(F32)
    ahead[...] = (lane == jnp.concatenate([column, column], axis=1)[:, :count]).astype(F32).astype(BF16)
    across[...] = (lax.broadcasted_iota(jnp.int32, (count, TILES), 0) == slots).astype(F32).astype(BF16)


def pick(picked, pieces, ahead, count):
    for m in range(VECS // 2):
        pair = pieces[:, 16 * m:16 * m + 16, :].astype(F32)
        even = pair[:, 0:8, :].reshape(count, TILE).astype(BF16)
        odd = pair[:, 8:16, :].reshape(count, TILE).astype(BF16)
        chosen = matmul(ahead[...], jnp.concatenate([even, odd], axis=1), NN)
        picked[pl.ds(2 * m, TILES, stride=VECS), :] = chosen[:, :TILE]
        picked[pl.ds(2 * m + 1, TILES, stride=VECS), :] = chosen[:, TILE:]


def place(terms, products, across, count):
    left = jnp.concatenate([across[...], across[...]], axis=1)
    for v in range(0, VECS, 2):
        columns = []
        for u in (v, v + 1):
            columns.append(jnp.concatenate(halves(products[pl.ds(u, TILES, stride=VECS), :]), axis=0))
        total = matmul(left, jnp.concatenate(columns, axis=1), NN)
        terms[:, 8 * v:8 * v + 8, :] = total[:, :TILE].reshape(count // 8, 8, TILE)
        terms[:, 8 * v + 8:8 * v + 16, :] = total[:, TILE:].reshape(count // 8, 8, TILE)


def multiply(products, picked, blocks):
    upper = lax.broadcasted_iota(jnp.int32, (16, TILE), 0) < 8

    def step(i, carry):
        for u in range(32):
            k = (i * 32 + u) * 2
            at = pl.ds(pl.multiple_of(k * 8, 16), 16)
            vectors = picked[at, :]
            left = jnp.concatenate(
                [jnp.where(upper, vectors, 0.0), jnp.where(upper, 0.0, vectors)], axis=1
            ).astype(BF16)
            products[at, :] = matmul(left, blocks[pl.ds(k, 2)].reshape(2 * TILE, TILE), NN)
        return carry

    lax.fori_loop(0, TILES // 64, step, 0)


def with_stack(sums, others, own):
    left, first, second = [], [], []
    for p in range(sums.shape[0]):
        for t in range(8):
            left.append(jnp.concatenate(halves(sums[p, pl.ds(t, VECS, stride=8), :]), axis=0))
            first.append(others[p, 16 * t:16 * t + 16, :])
            second.append(own[p, 8 * t:8 * t + 8, :].astype(BF16))
    left = jnp.concatenate(left, axis=1)
    first = matmul(left, jnp.concatenate(first, axis=1), NT)
    second = matmul(left, jnp.concatenate(second, axis=1), NT)
    both = jnp.concatenate([first, second], axis=1)
    return both[0:8] + both[8:16]


def pack(values):
    line = lax.broadcasted_iota(jnp.int32, (VECS, TILE), 0) % 4
    moved = jnp.where(line == 0, values, 0.0)
    for j in range(1, 4):
        moved = moved + jnp.where(line == j, pltpu.roll(values, 32 * j, axis=1), 0.0)
    return jnp.concatenate(
        [jnp.sum(moved[0:4], axis=0, keepdims=True), jnp.sum(moved[4:8], axis=0, keepdims=True)], axis=0
    )


def unpack(values):
    line = lax.broadcasted_iota(jnp.int32, (VECS, TILE), 0) % 4
    spread = jnp.concatenate(
        [jnp.broadcast_to(values[0:1], (4, TILE)), jnp.broadcast_to(values[1:2], (4, TILE))], axis=0
    )
    moved = jnp.where(line == 0, spread, 0.0)
    for j in range(1, 4):
        moved = moved + jnp.where(line == j, pltpu.roll(spread, TILE - 32 * j, axis=1), 0.0)
    return moved


def tree(terms):
    while len(terms) > 1:
        terms = [a + b for a, b in zip(terms[::2], terms[1::2])] + terms[len(terms) // 2 * 2:]
    return terms[0]


def by_tile(out, pieces, scratch):
    for p in range(out.shape[0]):
        scratch[...] = pieces[p].astype(F32)
        for t in range(8):
            out[p, 8 * t:8 * t + 8, :] = scratch[pl.ds(t, VECS, stride=8), :]


def kernel(
    tiles_hbm, row_hbm, col_hbm, basis_hbm, image_hbm, search_hbm, simage_hbm, ritz_hbm,
    ob, oi, opv,
    tiles, turned, row_v, col_v, ritz_s, work, images, pieces, scratch,
    ahead_r, across_r, ahead_c, across_c, picked, products,
    colbuf, rowbuf, others_c, others_r, own_c, own_r,
    rowterms, colterms, rowlow, ysib, rowsum, zlow, zr, csib, colsum, clow, cr,
    g_core, g_xy, g_yl, g_z, l_row, l_col,
    in_sem,
    cA_s, cA_r, cB_s, cB_r, zA_s, zA_r, yB_s, yB_r,
    oz_s, oz_r, on_s, on_r, oy_s, oy_r, ox_s, ox_r,
    ry_s, ry_r, rz_s, rz_r, sc_s, sc_r, sx_s, sx_r,
    gc_s, gc_r, gx_s, gx_r, gy_s, gy_r, gz_s, gz_r,
    lr_s, lr_r, ll_s, ll_r,
):
    row = lax.axis_index("row")
    col = lax.axis_index("col")
    xy, core = row // 2, row % 2
    yh, x = xy // N_X, xy % N_X
    z, yl = col // 2, col % 2
    sibling = (xy * 2 + 1 - core, col)
    across = (row, z * 2 + 1 - yl)

    def plane(dy, dx):
        return ((yh + dy) % N_YH) * N_X + (x + dx) % N_X

    def z_at(d):
        return (z + d) % N_Z

    def z_peer(d):
        return (row, z_at(d) * 2 + yl)

    def xy_peer(o):
        return (plane(*o) * 2 + core, col)

    def xy_from(o):
        return plane(N_YH - o[0], N_X - o[1])

    barrier = pltpu.get_barrier_semaphore()
    def col_peer(d, e):
        return (row, z_at(d) * 2 + (yl ^ e))

    everyone = [col_peer(d, e) for d, e in IN_COL] + [(row ^ d, col) for d in range(1, N_ROW)]
    for peer in everyone:
        pl.semaphore_signal(barrier, inc=1, device_id=peer, device_id_type=MESH)

    loads = [
        pltpu.make_async_copy(basis_hbm, work.at[pl.ds(0, 8)], in_sem.at[0]),
        pltpu.make_async_copy(image_hbm, work.at[pl.ds(24, 8)], in_sem.at[1]),
        pltpu.make_async_copy(ritz_hbm, ritz_s, in_sem.at[2]),
        pltpu.make_async_copy(search_hbm, work.at[pl.ds(16, 8)], in_sem.at[3]),
        pltpu.make_async_copy(simage_hbm, work.at[pl.ds(32, 8)], in_sem.at[4]),
        pltpu.make_async_copy(row_hbm, row_v, in_sem.at[5]),
        pltpu.make_async_copy(col_hbm, col_v, in_sem.at[6]),
        pltpu.make_async_copy(tiles_hbm.at[0, 0], tiles, in_sem.at[7]),
    ]
    for load in loads:
        load.start()
    for load in loads[:4]:
        load.wait()
    v_index = lax.broadcasted_iota(jnp.int32, (VECS, 1), 0)
    ritz = jnp.zeros((VECS, 1), F32)
    for v in range(VECS):
        ritz = jnp.where(v_index == v, ritz_s[v], ritz)
    residual = work[24:32, :] - ritz * work[0:8, :]
    work[8:16, :] = residual
    mine_col = core * N_XY + xy
    mine_row = yl * N_Z + z
    for t in range(8):
        cut = slice(t * TILE, (t + 1) * TILE)
        pieces[pl.ds(t, VECS, stride=8), :] = residual[:, cut]
        pair = jnp.concatenate([work[0:8, cut], work[16:24, cut]], axis=0).astype(BF16)
        others_c[xy, 16 * t:16 * t + 16, :] = pair
        others_r[z, 16 * t:16 * t + 16, :] = pair
    lowered = pieces[...].astype(BF16)
    colbuf[mine_col] = lowered
    rowbuf[mine_row] = lowered

    pl.semaphore_wait(barrier, len(everyone))

    sends = []

    def remote(src, dst, ss, rs, peer):
        return pltpu.make_async_remote_copy(
            src_ref=src, dst_ref=dst, send_sem=ss, recv_sem=rs, device_id=peer, device_id_type=MESH
        )

    def send(src, dst, ss, rs, peer):
        copy = remote(src, dst, ss, rs, peer)
        copy.start()
        sends.append(copy)

    def arrived(dst, ss, rs, peer):
        remote(dst, dst, ss, rs, peer).wait_recv()

    for d in Z_ORDER:
        send(rowbuf.at[mine_row], rowbuf.at[mine_row], zA_s.at[d], zA_r.at[d], z_peer(d))
    for j, o in enumerate(OFFSETS):
        send(colbuf.at[mine_col], colbuf.at[mine_col], cA_s.at[j], cA_r.at[j], xy_peer(o))
    send(rowbuf.at[mine_row], rowbuf.at[mine_row], yB_s.at[0], yB_r.at[0], across)

    def others_start():
        for d in (6, 3, 9):
            send(others_r.at[z], others_r.at[z], oz_s.at[d], oz_r.at[d], z_peer(d))
        for d in (2, 1, 3):
            send(others_c.at[xy], others_c.at[xy], oy_s.at[d], oy_r.at[d], xy_peer((d, 0)))
        for d in (2, 1, 3):
            send(others_c.at[xy], others_c.at[xy], ox_s.at[0, d], ox_r.at[0, d], xy_peer((0, d)))

    others_start()

    for load in loads[5:7]:
        load.wait()
    onehots(ahead_r, across_r, slots_of(row_v[0], N_Z), N_COL * 8)
    onehots(ahead_c, across_c, slots_of(col_v[0], N_XY), N_ROW * 8)

    loads[4].wait()
    given = dot_nt(work[0:24, :], work[0:40, :])
    g_core[core] = jnp.concatenate(
        [given[0:8], given[8:16], given[16:24], jnp.zeros((8, 8), F32)], axis=1
    )
    send(g_core.at[core], g_core.at[core], gc_s, gc_r, sibling)

    loads[7].wait()

    def turn(i, carry):
        for u in range(16):
            turned[i * 16 + u] = tiles[i * 16 + u].T
        return carry

    lax.fori_loop(0, TILES // 16, turn, 0)

    for dy in range(N_YH):
        for dx in range(N_X):
            if (dy, dx) != (0, 0):
                j = OFFSETS.index((dy, dx))
                arrived(colbuf.at[core * N_XY + xy_from((dy, dx))], cA_s.at[j], cA_r.at[j], xy_peer((dy, dx)))
        block = colbuf.at[pl.ds(core * N_XY + ((yh + N_YH - dy) % N_YH) * N_X, N_X)]
        send(block, block, cB_s.at[dy], cB_r.at[dy], sibling)
    for d in reversed(Z_ORDER):
        here = rowbuf.at[yl * N_Z + z_at(N_Z - d)]
        arrived(here, zA_s.at[d], zA_r.at[d], z_peer(d))
        send(here, here, yB_s.at[d], yB_r.at[d], across)

    def others_on():
        for d in (1, 3, 2):
            here = others_c.at[plane(N_YH - d, 0)]
            arrived(here, oy_s.at[d], oy_r.at[d], xy_peer((d, 0)))
            for e in (2, 1, 3):
                send(here, here, ox_s.at[d, e], ox_r.at[d, e], xy_peer((0, e)))

    others_on()
    for d in (0, 3, 9, 6):
        here = others_r.at[z_at(N_Z - d)]
        if d:
            arrived(here, oz_s.at[d], oz_r.at[d], z_peer(d))
        for e in (1, N_Z - 1):
            send(here, here, on_s.at[e // 2, d // 3], on_r.at[e // 2, d // 3], z_peer(e))

    arrived(g_core.at[1 - core], gc_s, gc_r, sibling)
    g_xy[xy] = g_core[0] + g_core[1]
    for j, o in enumerate(OFFSETS):
        send(g_xy.at[xy], g_xy.at[xy], gx_s.at[j], gx_r.at[j], xy_peer(o))

    for dy in range(N_YH):
        block = colbuf.at[pl.ds((1 - core) * N_XY + ((yh + N_YH - dy) % N_YH) * N_X, N_X)]
        arrived(block, cB_s.at[dy], cB_r.at[dy], sibling)
    pick(picked, colbuf, ahead_c, N_ROW * 8)
    multiply(products, picked, turned)
    place(rowterms, products, across_r, N_COL * 8)
    for q in range(2):
        half = pl.ds(q * N_Z // 2, N_Z // 2)
        rowlow[half] = rowterms[pl.ds((1 - yl) * N_Z + q * N_Z // 2, N_Z // 2)].astype(BF16)
        send(rowlow.at[half], ysib.at[half], ry_s.at[q], ry_r.at[q], across)

    for d in range(N_Z):
        arrived(rowbuf.at[(1 - yl) * N_Z + z_at(N_Z - d)], yB_s.at[d], yB_r.at[d], across)
    pick(picked, rowbuf, ahead_r, N_COL * 8)
    multiply(products, picked, tiles)
    place(colterms, products, across_c, N_ROW * 8)
    chunk = N_XY // 4
    for q in range(4):
        send(
            colterms.at[pl.ds((1 - core) * N_XY + q * chunk, chunk)],
            csib.at[pl.ds(q * chunk, chunk)], sc_s.at[q], sc_r.at[q], sibling,
        )

    for j, o in enumerate(OFFSETS):
        arrived(g_xy.at[xy_from(o)], gx_s.at[j], gx_r.at[j], xy_peer(o))
    total = g_xy[0]
    for j in range(1, N_XY):
        total = total + g_xy[j]
    g_yl[yl] = total
    send(g_yl.at[yl], g_yl.at[yl], gy_s, gy_r, across)
    by_tile(own_c, colbuf.at[pl.ds(core * N_XY, N_XY)], scratch)
    by_tile(own_r, rowbuf.at[pl.ds(yl * N_Z, N_Z)], scratch)

    for q in range(4):
        at = pl.ds(q * chunk, chunk)
        arrived(csib.at[at], sc_s.at[q], sc_r.at[q], sibling)
        both = colterms[pl.ds(core * N_XY + q * chunk, chunk)] + csib[at]
        colsum[at] = both
        clow[at] = both.astype(BF16)
    for j, o in enumerate(OFFSETS):
        send(clow.at[plane(*o)], cr.at[xy], sx_s.at[j], sx_r.at[j], xy_peer(o))
    arrived(g_yl.at[1 - yl], gy_s, gy_r, across)
    g_z[z] = g_yl[0] + g_yl[1]
    for d in Z_ORDER:
        send(g_z.at[z], g_z.at[z], gz_s.at[d], gz_r.at[d], z_peer(d))
    for d in (1, 2, 3):
        for e in range(N_YH):
            arrived(others_c.at[plane(N_YH - e, N_X - d)], ox_s.at[e, d], ox_r.at[e, d], xy_peer((0, d)))
    in_plane = with_stack(colsum, others_c, own_c)
    for q in range(2):
        half = pl.ds(q * N_Z // 2, N_Z // 2)
        arrived(ysib.at[half], ry_s.at[q], ry_r.at[q], across)
        both = rowterms[pl.ds(yl * N_Z + q * N_Z // 2, N_Z // 2)] + ysib[half].astype(F32)
        rowsum[half] = both
        zlow[half] = both.astype(BF16)
    for d in Z_ORDER:
        send(zlow.at[z_at(d)], zr.at[z], rz_s.at[d], rz_r.at[d], z_peer(d))
    for d in (0, 3, 9, 6):
        for e in (1, N_Z - 1):
            arrived(others_r.at[z_at(2 * N_Z - d - e)], on_s.at[e // 2, d // 3], on_r.at[e // 2, d // 3], z_peer(e))
    last = in_plane + with_stack(rowsum, others_r, own_r)
    l_row[row] = pack(jnp.concatenate([last, jnp.zeros((VECS, TILE - 24), F32)], axis=1))
    for d in range(1, N_ROW):
        send(l_row.at[row], l_row.at[row], lr_s.at[d], lr_r.at[d], (row ^ d, col))

    for d in range(1, N_ROW):
        arrived(l_row.at[row ^ d], lr_s.at[d], lr_r.at[d], (row ^ d, col))
    l_col[col] = tree([l_row[j] for j in range(N_ROW)])
    for d, e in IN_COL:
        send(l_col.at[col], l_col.at[col], ll_s.at[d, e], ll_r.at[d, e], col_peer(d, e))

    for d in Z_ORDER:
        arrived(g_z.at[z_at(N_Z - d)], gz_s.at[d], gz_r.at[d], z_peer(d))
    total = g_z[0]
    for j in range(1, N_Z):
        total = total + g_z[j]
    n_total = F32(1024 * N_ROW * N_COL)
    total = total / n_total
    total = jnp.concatenate([total[:, 0:40], total[:, 40:80], total[:, 80:120]], axis=0)
    rows = lax.broadcasted_iota(jnp.int32, (24, 24), 0)
    columns = lax.broadcasted_iota(jnp.int32, (24, 24), 1)
    matrix = jnp.concatenate([total[:, 0:24], jnp.where(rows == columns, F32(1.0), F32(0.0))], axis=1)
    index = lax.broadcasted_iota(jnp.int32, (24, 1), 0)
    for step in range(24):
        pivot = jnp.sqrt(matrix[step:step + 1, step:step + 1])
        scaled = matrix[step:step + 1, :] / pivot
        factor = matrix[:, step:step + 1] / pivot
        matrix = jnp.where(
            index == step, scaled, jnp.where(index > step, matrix - factor * scaled, matrix)
        )
    inverse = matrix[:, 24:48]
    reordered = jnp.concatenate([inverse[:, 0:8], inverse[:, 16:24], inverse[:, 8:16]], axis=1)
    given = dot_nt(dot_nn(inverse, total[:, 24:32]), inverse[:, 0:8]) + dot_nt(
        dot_nn(inverse, total[:, 32:40]), inverse[:, 16:24]
    )
    ob[...] = dot_nn(inverse, work[0:24, :])

    image = rowsum[z] + colsum[xy]
    for d in reversed(Z_ORDER):
        arrived(zr.at[z_at(N_Z - d)], rz_s.at[d], rz_r.at[d], z_peer(d))
        image = image + zr[z_at(N_Z - d)].astype(F32)
    for j, o in enumerate(OFFSETS):
        arrived(cr.at[xy_from(o)], sx_s.at[j], sx_r.at[j], xy_peer(o))
        image = image + cr[xy_from(o)].astype(F32)
    pieces[...] = image
    for t in range(8):
        images[8:16, t * TILE:(t + 1) * TILE] = pieces[pl.ds(t, VECS, stride=8), :]
    images[0:8, :] = work[24:32, :]
    images[16:24, :] = work[32:40, :]
    oi[...] = dot_nn(inverse, images[...])

    for d, e in IN_COL:
        arrived(l_col.at[z_at(N_Z - d) * 2 + (yl ^ e)], ll_s.at[d, e], ll_r.at[d, e], col_peer(d, e))
    late = unpack(tree([l_col[j] for j in range(N_COL)])) / n_total
    opv[...] = given + dot_nt(dot_nt(reordered, late[:, 0:24]), inverse[:, 8:16])
    for copy in sends:
        copy.wait_send()


def on_device(tiles, tile_row, tile_col, basis, basis_image, search, search_image, ritz_values):
    vmem, dma = pltpu.VMEM, pltpu.SemaphoreType.DMA
    n_off = N_XY - 1
    outs = (
        jax.ShapeDtypeStruct((24, 1024), F32),
        jax.ShapeDtypeStruct((24, 1024), F32),
        jax.ShapeDtypeStruct((24, 24), F32),
    )

    def pairs(*shapes):
        return [dma(shape) for shape in shapes for _ in range(2)]

    results = pl.pallas_call(
        kernel,
        out_shape=tuple(vmem(out.shape, F32) for out in outs),
        in_specs=[pl.BlockSpec(memory_space=pl.ANY)] * 8,
        out_specs=[pl.BlockSpec(memory_space=vmem)] * 3,
        scratch_shapes=[
            vmem((TILES, TILE, TILE), BF16),
            vmem((TILES, TILE, TILE), BF16),
            vmem((1, 1, TILES), jnp.int32),
            vmem((1, 1, TILES), jnp.int32),
            pltpu.SMEM((VECS,), F32),
            vmem((40, 1024), F32),
            vmem((24, 1024), F32),
            vmem((64, TILE), F32),
            vmem((64, TILE), F32),
            vmem((TILES, N_COL * 8), BF16),
            vmem((N_COL * 8, TILES), BF16),
            vmem((TILES, N_ROW * 8), BF16),
            vmem((N_ROW * 8, TILES), BF16),
            vmem((TILES * VECS, TILE), F32),
            vmem((TILES * VECS, TILE), F32),
            vmem((N_ROW, 64, TILE), BF16),
            vmem((N_COL, 64, TILE), BF16),
            vmem((N_XY, 128, TILE), BF16),
            vmem((N_Z, 128, TILE), BF16),
            vmem((N_XY, 64, TILE), F32),
            vmem((N_Z, 64, TILE), F32),
            vmem((N_COL, 64, TILE), F32),
            vmem((N_ROW, 64, TILE), F32),
            vmem((N_Z, 64, TILE), BF16),
            vmem((N_Z, 64, TILE), BF16),
            vmem((N_Z, 64, TILE), F32),
            vmem((N_Z, 64, TILE), BF16),
            vmem((N_Z, 64, TILE), BF16),
            vmem((N_XY, 64, TILE), F32),
            vmem((N_XY, 64, TILE), F32),
            vmem((N_XY, 64, TILE), BF16),
            vmem((N_XY, 64, TILE), BF16),
            vmem((2, 8, TILE), F32),
            vmem((N_XY, 8, TILE), F32),
            vmem((2, 8, TILE), F32),
            vmem((N_Z, 8, TILE), F32),
            vmem((N_ROW, 2, TILE), F32),
            vmem((N_COL, 2, TILE), F32),
            dma((8,)),
        ] + pairs(
            (n_off,), (N_YH,), (N_Z,), (N_Z,), (N_Z,), (6, 4), (N_YH,), (N_YH, N_X),
            (2,), (N_Z,), (4,), (n_off,),
            (), (n_off,), (), (N_Z,), (N_ROW,), (N_Z, 2),
        ),
        compiler_params=pltpu.CompilerParams(
            collective_id=0, has_side_effects=True, vmem_limit_bytes=56 * 2**20
        ),
        name="step",
    )(tiles, tile_row, tile_col, basis, basis_image, search, search_image, ritz_values)
    return tuple(results)


def solution(mesh):
    vectors = P(None, ("row", "col"))
    return jax.shard_map(
        on_device,
        mesh=mesh,
        in_specs=(
            P("row", "col", None, None, None),
            P("row", "col", None),
            P("row", "col", None),
            vectors, vectors, vectors, vectors,
            P(),
        ),
        out_specs=(vectors, vectors, P()),
        check_vma=False,
    )
```
